256 devices in a mesh: dp: 4 (over y), space: 64 (over z, x, core).
Axes of the slice: x: 4, y: 4, z: 8, core: 2. Of those that a mesh axis runs over, the one named last changes fastest.
Arguments:
- features: bfloat16 [4, 16384, 256], P('dp', 'space'), may hold values from -6 to 6
- neighbours: int32 [4, 27, 16384], P('dp', None, 'space'), may hold values from -1 to 16383, as said below
- parents: int32 [4, 16384], P('dp', 'space'), may hold values from 0 to 4095, as said below
- conv_first: bfloat16 [27, 256, 256], replicated, may hold values from -0.078125 to 0.078125
- conv_second: bfloat16 [27, 256, 256], replicated, may hold values from -0.078125 to 0.078125
- gain_first: float32 [256], replicated, may hold values from 0.1 to 1.9
- gain_second: float32 [256], replicated, may hold values from 0.1 to 1.9
- down_weight: bfloat16 [256, 512], replicated, may hold values from -0.375 to 0.375
- cotangent: bfloat16 [4, 4096, 512], P('dp', 'space'), may hold values from -6 to 6
Outputs:
- fine_out: bfloat16 [4, 16384, 256], P('dp', 'space')
- coarse: bfloat16 [4, 4096, 512], P('dp', 'space')
- down_grad: float32 [256, 512], replicated
The draws below stay inside these ranges and needn't reach their ends.
Inputs may be any that keep to these rules, and one draw needn't show every extreme that they name: `neighbours`: for a site s of the block [d * 256, (d + 1) * 256), every entry is -1 or lies in [(d - 1) * 256, (d + 2) * 256); entry 13 is s itself. The parents of the sites of the block [d * 256, (d + 1) * 256) never decrease along the block and lie in [d * 64, (d + 2) * 64).
All inputs are finite; a program needn't handle non-finite values.
Results may differ from the reference program's by a relative error of at most 0.0057.
Values may be sent and summed in bfloat16 or wider, within the bound.
No kernel may reach another device: no remote copies, remote signals or barrier semaphores. Data moves between devices by JAX's collectives and lax.ppermute only.
A program may use at most 64 MiB of HBM per device.

```python
import math
import jax
import jax.numpy as jnp
from jax import lax

CH = 256
CH_OUT = 512
TAPS = 27
SITE_DEV = 256
PAR_DEV = 64
SITES = 16384
PARENTS = 4096
WORLDS = 4
N_SPACE = 64


def draw_neighbours(key, part):
    first_key, second_key = jax.random.split(jax.random.fold_in(key, 11))
    site_ids = jnp.arange(SITES, dtype=jnp.int32)
    lowest = (site_ids // SITE_DEV - 1) * SITE_DEV
    offsets = jax.random.randint(first_key, (WORLDS, TAPS, SITES), 0, 3 * SITE_DEV)
    global_ids = lowest[None, None, :] + offsets
    alive = jax.random.randint(second_key, (WORLDS, TAPS, SITES), 0, 10) >= 3
    inside = (global_ids >= 0) & (global_ids < SITES)
    global_ids = jnp.where(alive & inside, global_ids, -1)
    centre = (jnp.arange(TAPS) == 13)[None, :, None]
    return jnp.where(centre, site_ids[None, None, :], global_ids).astype(jnp.int32)


def draw_parents(key, part):
    first_key, second_key = jax.random.split(jax.random.fold_in(key, 23))
    extent = jax.random.randint(first_key, (WORLDS, N_SPACE), PAR_DEV // 2, 2 * PAR_DEV + 1)
    extent = extent.at[:, 0].set(2 * PAR_DEV)
    final = (jnp.arange(N_SPACE) == N_SPACE - 1)[None, :]
    extent = jnp.where(final, jnp.minimum(extent, PAR_DEV), extent)
    draws_raw = jax.random.randint(second_key, (WORLDS, N_SPACE, SITE_DEV), 0, 2 * PAR_DEV)
    offsets = jnp.sort(draws_raw % extent[:, :, None], axis=-1)
    offsets = offsets.at[:, :, -1].set(extent - 1)
    anchor = (jnp.arange(N_SPACE, dtype=jnp.int32) * PAR_DEV)[None, :, None]
    return (anchor + offsets).reshape(WORLDS, SITES).astype(jnp.int32)


def steps_of(stream_key, shape, shards, least, top_value):
    def one(dim, shards_of):
        steps = jax.random.uniform(jax.random.fold_in(jax.random.fold_in(stream_key, 6), dim), (shards_of,), jnp.float32, least / len(shards), top_value / len(shards))
        return jnp.repeat(jnp.exp(steps), shape[dim] // shards_of).reshape((-1,) + (1,) * (len(shape) - dim - 1))

    level = one(*shards[0])
    for cut in shards[1:]:
        level = level * one(*cut)
    return level


def scatter_about(key, dims, deviation, limit, cuts=(), kind=jnp.bfloat16):
    result = jax.random.normal(key, dims, jnp.float32) * deviation
    if len(cuts) > 0:
        result = steps_of(key, dims, cuts, -0.22, 0.18) * result
    return jnp.clip(result, min=-limit, max=limit).astype(kind)


def setup_inputs(seed: int = 0) -> dict:
    keys = jax.random.split(jax.random.key(seed), 10)
    return {
        "features": scatter_about(keys[0], (WORLDS, SITES, CH), 1.0, 6.0, ((0, 4), (1, 64))),
        "neighbours": draw_neighbours(jax.random.fold_in(keys[9], 71), 0),
        "parents": draw_parents(jax.random.fold_in(keys[9], 71), 0),
        "conv_first": scatter_about(keys[3], (TAPS, CH, CH), (TAPS * CH) ** -0.5, 0.078125),
        "conv_second": scatter_about(keys[4], (TAPS, CH, CH), (TAPS * CH) ** -0.5, 0.078125),
        "gain_first": jnp.clip(1.0 + 0.18 * jax.random.normal(keys[5], (CH,), jnp.float32), 0.1, 1.9),
        "gain_second": jnp.clip(1.0 + 0.18 * jax.random.normal(keys[6], (CH,), jnp.float32), 0.1, 1.9),
        "down_weight": scatter_about(keys[7], (CH, CH_OUT), CH ** -0.5, 0.375),
        "cotangent": scatter_about(keys[8], (WORLDS, PARENTS, CH_OUT), 1.0, 6.0, ((0, 4), (1, 64))),
    }


def convolve(field, tap_lists, weights):
    site_rows = field.shape[0]
    padded = jnp.concatenate([field, jnp.zeros((1, field.shape[1]), field.dtype)], axis=0)
    lookup = jnp.where(tap_lists < 0, site_rows, tap_lists).astype(jnp.int32)

    def one_tap(running, inputs):
        rows_now, weight = inputs
        return (running + jnp.dot(padded[rows_now], weight, preferred_element_type=jnp.float32), None)
    start = jnp.zeros((site_rows, weights.shape[2]), jnp.float32)
    running, _ = lax.scan(one_tap, start, (lookup, weights))
    return running

def settle(running, gain):
    inverse = lax.rsqrt(lax.optimization_barrier(jnp.mean(running * running, axis=-1, keepdims=True)) + 1e-05)
    return jax.nn.silu(running * inverse * gain)

def reference(features, neighbours, parents, conv_first, conv_second, gain_first, gain_second, down_weight, cotangent):

    def one_world(inputs):
        field, tap_lists, parent_ids, grad_in = inputs
        middle = settle(convolve(field, tap_lists, conv_first), gain_first).astype(jnp.bfloat16)
        fine_out = (field.astype(jnp.float32) + settle(convolve(middle, tap_lists, conv_second), gain_second)).astype(jnp.bfloat16)
        parent_sums = jax.ops.segment_sum(fine_out.astype(jnp.float32), parent_ids, num_segments=PARENTS)
        counts = jax.ops.segment_sum(jnp.ones(parent_ids.shape, jnp.float32), parent_ids, num_segments=PARENTS)
        pooled = (parent_sums / jnp.maximum(counts, 1.0)[:, None]).astype(jnp.bfloat16)
        coarse = jnp.dot(pooled, down_weight, preferred_element_type=jnp.float32).astype(jnp.bfloat16)
        local_grad = jnp.dot(pooled.T, grad_in, preferred_element_type=jnp.float32)
        return (fine_out, coarse, local_grad)
    fine_out, coarse, grads = lax.map(one_world, (features, neighbours, parents, cotangent))
    down_grad = lax.optimization_barrier(jnp.sum(grads, axis=0)) * (1.0 / math.sqrt(WORLDS * PARENTS))
    return (fine_out, coarse, down_grad)
```

```python
import math

import jax
import jax.numpy as jnp
from jax import lax
from jax.sharding import Mesh
from jax.sharding import PartitionSpec as P


DP = "y"
SPACE = ("z", "x", "core")
PLANE = ("y", "x", "core")


def split_mesh(mesh):
    dp, space = mesh.devices.shape
    return Mesh(mesh.devices.reshape(dp, space // 8, 4, 2), (DP,) + SPACE)


def extended(cells, sides, width):
    for axis, dim in sides:
        count = lax.axis_size(axis)
        ends = count - 1
        head = lax.slice_in_dim(cells, 0, width, axis=dim)
        tail = lax.slice_in_dim(cells, cells.shape[dim] - width, cells.shape[dim], axis=dim)
        cells = jnp.concatenate(
            [
                lax.ppermute(tail, axis, [(i, (i + 1) % count) for i in range(ends)]),
                cells,
                lax.ppermute(head, axis, [((i + 1) % count, i) for i in range(ends)]),
            ],
            axis=dim,
        )
    return cells


def from_behind(array, axis, by):
    length = lax.axis_size(axis)
    pairs = [(i, i + by) for i in range(length) if 0 <= i + by < length]
    return lax.ppermute(array, axis, pairs)


def convolve(field, tap_lists, weights):
    site_rows = field.shape[1]
    nearby = extended(field, ((SPACE, 1),), site_rows)
    lowest = (lax.axis_index(SPACE) - 1) * site_rows
    lookup = jnp.where(tap_lists < 0, 3 * site_rows, tap_lists - lowest)
    window_ids = jnp.arange(3 * site_rows, dtype=jnp.int32)

    def one_tap(running, inputs):
        rows_now, weight = inputs
        selector = (rows_now[:, :, None] == window_ids[None, None, :]).astype(jnp.bfloat16)
        picked = jnp.einsum(
            "wsr,wrc->wsc", selector, nearby, preferred_element_type=jnp.float32
        ).astype(jnp.bfloat16)
        return (
            running + jnp.einsum("wsc,cd->wsd", picked, weight, preferred_element_type=jnp.float32),
            None,
        )

    start = jnp.zeros((field.shape[0], site_rows, weights.shape[2]), jnp.float32)
    running, _ = lax.scan(one_tap, start, (jnp.moveaxis(lookup, 1, 0), weights))
    return running


def settle(running, gain):
    inverse = lax.rsqrt(jnp.mean(running * running, axis=-1, keepdims=True) + 1e-05)
    return jax.nn.silu(running * inverse * gain)


def exchanged(pieces, axes):
    return lax.all_to_all(pieces, axes, 0, 0, tiled=True)


def reduced(local_grad, scale):
    rows, cols = local_grad.shape
    plane = lax.axis_size(PLANE)
    parts = local_grad.astype(jnp.bfloat16).reshape(plane, rows // plane, cols)
    part = jnp.sum(exchanged(parts, PLANE).astype(jnp.float32), axis=0)
    copies = jnp.broadcast_to(part[None], (lax.axis_size("z"),) + part.shape)
    part = jnp.sum(exchanged(copies, "z"), axis=0) * scale
    copies = jnp.broadcast_to(part.astype(jnp.bfloat16)[None], (plane,) + part.shape)
    return exchanged(copies, PLANE).astype(jnp.float32).reshape(rows, cols)


def body(
    features,
    neighbours,
    parents,
    conv_first,
    conv_second,
    gain_first,
    gain_second,
    down_weight,
    cotangent,
):
    middle = settle(convolve(features, neighbours, conv_first), gain_first).astype(jnp.bfloat16)
    fine_out = (
        features.astype(jnp.float32)
        + settle(convolve(middle, neighbours, conv_second), gain_second)
    ).astype(jnp.bfloat16)
    par_rows = cotangent.shape[1]
    owner_id = lax.axis_index(SPACE)
    world_rows = features.shape[0]
    parent_ids = owner_id * par_rows + jnp.arange(2 * par_rows, dtype=jnp.int32)
    onehot = (parents[:, None, :] == parent_ids[None, :, None]).astype(jnp.bfloat16)
    partial_value = jnp.einsum("wps,wsc->wpc", onehot, fine_out, preferred_element_type=jnp.float32)
    tallies = jnp.sum(onehot.astype(jnp.float32), axis=2)
    moved = from_behind((partial_value[:, par_rows:], tallies[:, par_rows:]), SPACE, 1)
    parent_sums = partial_value[:, :par_rows] + moved[0]
    counts = tallies[:, :par_rows] + moved[1]
    pooled = (parent_sums / jnp.maximum(counts, 1.0)[:, :, None]).astype(jnp.bfloat16)
    coarse = jnp.einsum(
        "wpc,cd->wpd", pooled, down_weight, preferred_element_type=jnp.float32
    ).astype(jnp.bfloat16)
    local_grad = jnp.einsum("wpc,wpd->cd", pooled, cotangent, preferred_element_type=jnp.float32)
    worlds_all = world_rows * lax.axis_size(DP)
    parents_all = par_rows * lax.axis_size(SPACE)
    down_grad = reduced(local_grad, 1.0 / math.sqrt(worlds_all * parents_all))
    return (fine_out, coarse, down_grad)


def solution(mesh):
    return jax.shard_map(
        body,
        mesh=split_mesh(mesh),
        in_specs=(
            P(DP, SPACE, None),
            P(DP, None, SPACE),
            P(DP, SPACE),
            P(),
            P(),
            P(),
            P(),
            P(),
            P(DP, SPACE, None),
        ),
        out_specs=(P(DP, SPACE, None), P(DP, SPACE, None), P()),
        check_vma=False,
    )
```

```python
import functools
import math

import jax
import jax.numpy as jnp
from jax import lax
from jax.experimental import pallas as pl
from jax.experimental.pallas import tpu as pltpu
from jax.sharding import Mesh
from jax.sharding import PartitionSpec as P


DP = "y"
SPACE = ("z", "x", "core")
PLANE = ("y", "x", "core")
GROUP = 3
VMEM_BYTES = 40 << 20


def split_mesh(mesh):
    dp, space = mesh.devices.shape
    return Mesh(mesh.devices.reshape(dp, space // 8, 4, 2), (DP,) + SPACE)


def shifted(array, by):
    length = lax.axis_size(SPACE)
    return lax.ppermute(array, SPACE, [(i, (i + by) % length) for i in range(length)])


def settled(running, gain):
    inverse = lax.rsqrt(jnp.mean(running * running, axis=-1, keepdims=True) + 1e-05)
    scaled = running * inverse * gain
    return scaled / (1.0 + jnp.exp(-scaled))


def convolved(taps_ref, blocks, weight_ref, select_ref, picked_ref):
    taps, rows = taps_ref.shape
    chans = picked_ref.shape[1] // taps
    window = 3 * rows
    lowest = (lax.axis_index(SPACE) - 1) * rows
    ids = taps_ref[...]
    local = jnp.where(ids < 0, -1, ids - lowest)
    local = jnp.concatenate([local, jnp.full((-taps % 8, rows), -1, jnp.int32)], axis=0).T
    places = lax.broadcasted_iota(jnp.int16, (rows, window), 1)
    for tap in range(taps):
        wanted = jnp.broadcast_to(local[:, tap : tap + 1], (rows, 128)).astype(jnp.int16)
        wanted = jnp.concatenate([wanted] * (window // 128), axis=1)
        select_ref[tap * rows : (tap + 1) * rows] = jnp.where(
            wanted == places, jnp.ones((), jnp.bfloat16), jnp.zeros((), jnp.bfloat16)
        )
    for first in range(0, taps, GROUP):
        part = select_ref[first * rows : (first + GROUP) * rows]
        picked = sum(
            jnp.dot(
                part[:, b * rows : (b + 1) * rows], block[...], preferred_element_type=jnp.float32
            )
            for b, block in enumerate(blocks)
        ).astype(jnp.bfloat16)
        for j in range(GROUP):
            picked_ref[:, (first + j) * chans : (first + j + 1) * chans] = picked[j * rows : (j + 1) * rows]
    return jnp.dot(
        picked_ref[...],
        weight_ref[...].reshape(taps * chans, weight_ref.shape[2]),
        preferred_element_type=jnp.float32,
    )


def first_kernel(before, here, after, taps_ref, gain_ref, weight_ref, out, select_ref, picked_ref):
    product = convolved(taps_ref, (before, here, after), weight_ref, select_ref, picked_ref)
    out[...] = settled(product, gain_ref[...]).astype(out.dtype)


def second_kernel(
    before, here, after, taps_ref, gain_ref, weight_ref, feature_ref, parent_ref,
    fine_ref, own_ref, sent_ref, select_ref, picked_ref,
):
    product = convolved(taps_ref, (before, here, after), weight_ref, select_ref, picked_ref)
    fine = feature_ref[...].astype(jnp.float32) + settled(product, gain_ref[...])
    fine = fine.astype(fine_ref.dtype)
    fine_ref[...] = fine
    half, chans = own_ref.shape[0], fine.shape[1]
    ids = parent_ref[...] - lax.axis_index(SPACE) * half
    member = lax.broadcasted_iota(jnp.int32, (2 * half, fine.shape[0]), 0) == ids
    member = member.astype(jnp.float32)
    sums = jnp.dot(member.astype(jnp.bfloat16), fine, preferred_element_type=jnp.float32)
    counts = jnp.broadcast_to(jnp.sum(member, axis=1, keepdims=True), (2 * half, 128))
    own_ref[:, :chans] = sums[:half]
    own_ref[:, chans:] = counts[:half]
    sent_ref[:, :chans] = sums[half:]
    sent_ref[:, chans:] = counts[half:]


def coarse_kernel(own_ref, moved_ref, down_ref, cotangent_ref, coarse_ref, grad_ref):
    total = own_ref[...] + moved_ref[...]
    chans = down_ref.shape[0]
    counts = jnp.maximum(total[:, chans : chans + 1], 1.0)
    pooled = (total[:, :chans] / counts).astype(jnp.bfloat16)
    coarse_ref[...] = jnp.dot(pooled, down_ref[...], preferred_element_type=jnp.float32).astype(coarse_ref.dtype)
    grad_ref[...] = lax.dot_general(
        pooled, cotangent_ref[...], (((0,), (0,)), ((), ())), preferred_element_type=jnp.float32
    ).astype(grad_ref.dtype)


def in_vmem(kernel, outs, inputs, scratch=(), name=None):
    vmem = pl.BlockSpec(memory_space=pltpu.VMEM)
    return pl.pallas_call(
        kernel,
        out_shape=outs,
        in_specs=[vmem] * len(inputs),
        out_specs=jax.tree.map(lambda _: vmem, outs),
        scratch_shapes=scratch,
        compiler_params=pltpu.CompilerParams(vmem_limit_bytes=VMEM_BYTES),
        name=name,
    )(*inputs)


def exchanged(pieces, axes):
    return lax.all_to_all(pieces, axes, 0, 0, tiled=True)


def reduced(local_grad, scale):
    rows, cols = local_grad.shape
    plane = lax.axis_size(PLANE)
    parts = local_grad.reshape(plane, rows // plane, cols)
    part = jnp.sum(exchanged(parts, PLANE).astype(jnp.float32), axis=0)
    copies = jnp.broadcast_to(part[None], (lax.axis_size("z"),) + part.shape)
    part = jnp.sum(exchanged(copies, "z"), axis=0) * scale
    copies = jnp.broadcast_to(part.astype(jnp.bfloat16)[None], (plane,) + part.shape)
    return exchanged(copies, PLANE).astype(jnp.float32).reshape(rows, cols)


def body(
    features,
    neighbours,
    parents,
    conv_first,
    conv_second,
    gain_first,
    gain_second,
    down_weight,
    cotangent,
):
    field, taps_ids, grad_in = features[0], neighbours[0], cotangent[0]
    taps, rows = taps_ids.shape
    chans = field.shape[1]
    par_rows, out_chans = grad_in.shape
    bf16 = functools.partial(jax.ShapeDtypeStruct, dtype=jnp.bfloat16)
    f32 = functools.partial(jax.ShapeDtypeStruct, dtype=jnp.float32)
    scratch = [
        pltpu.VMEM((taps * rows, 3 * rows), jnp.bfloat16),
        pltpu.VMEM((rows, taps * chans), jnp.bfloat16),
    ]
    middle = in_vmem(
        first_kernel,
        bf16((rows, chans)),
        (shifted(field, 1), field, shifted(field, -1), taps_ids, gain_first[None], conv_first),
        scratch,
        "first_conv",
    )
    fine, own, sent = in_vmem(
        second_kernel,
        (bf16((rows, chans)), f32((par_rows, chans + 128)), f32((par_rows, chans + 128))),
        (
            shifted(middle, 1), middle, shifted(middle, -1), taps_ids, gain_second[None], conv_second,
            field, parents,
        ),
        scratch,
        "second_conv",
    )
    coarse, local_grad = in_vmem(
        coarse_kernel,
        (bf16((par_rows, out_chans)), bf16((chans, out_chans))),
        (own, shifted(sent, 1), down_weight, grad_in),
        name="coarse",
    )
    worlds_all = lax.axis_size(DP)
    parents_all = par_rows * lax.axis_size(SPACE)
    down_grad = reduced(local_grad, 1.0 / math.sqrt(worlds_all * parents_all))
    return (fine[None], coarse[None], down_grad)


def solution(mesh):
    return jax.shard_map(
        body,
        mesh=split_mesh(mesh),
        in_specs=(
            P(DP, SPACE, None),
            P(DP, None, SPACE),
            P(DP, SPACE),
            P(),
            P(),
            P(),
            P(),
            P(),
            P(DP, SPACE, None),
        ),
        out_specs=(P(DP, SPACE, None), P(DP, SPACE, None), P()),
        check_vma=False,
    )
```

```python
import functools
import math

import jax
import jax.numpy as jnp
from jax import lax
from jax.experimental import pallas as pl
from jax.experimental.pallas import tpu as pltpu
from jax.sharding import Mesh
from jax.sharding import PartitionSpec as P


DP = "y"
SPACE = ("z", "x", "core")
PLANE = ("y", "x", "core")
GROUP = 3
VMEM_BYTES = 32 << 20
PAR_ROWS = 64
COST_BYTES = 1 << 20


def split_mesh(mesh):
    dp, space = mesh.devices.shape
    return Mesh(mesh.devices.reshape(dp, space // 8, 4, 2), (DP,) + SPACE)


def shifted(array, by):
    length = lax.axis_size(SPACE)
    return lax.ppermute(array, SPACE, [(i, i + by) for i in range(length) if 0 <= i + by < length])


def from_partner(array):
    length = lax.axis_size(SPACE)
    return lax.ppermute(array, SPACE, [(i, i ^ 1) for i in range(length)])


def from_across(array):
    last = lax.axis_size(SPACE) - 1
    pairs = [(i, i + 1) for i in range(1, last, 2)]
    return lax.ppermute(array, SPACE, pairs + [(j, i) for i, j in pairs])


def settled(running, gain):
    inverse = lax.rsqrt(jnp.mean(running * running, axis=-1, keepdims=True) + 1e-05)
    scaled = running * inverse * gain
    return scaled / (1.0 + jnp.exp(-scaled))


def local_table(taps_ref):
    taps, _, rows = taps_ref.shape
    lowest = (lax.axis_index(SPACE) - 1) * rows
    ids = taps_ref[...].reshape(taps, rows)
    local = jnp.where(ids < 0, -4 * rows, ids - lowest)
    return jnp.concatenate([local, jnp.full((-taps % 8, rows), -1, jnp.int32)], axis=0).T


def pick(local, taps, blocks, select_ref, put):
    rows = local.shape[0]
    places = lax.broadcasted_iota(jnp.int16, (rows, rows), 1)
    one, zero = jnp.ones((), jnp.bfloat16), jnp.zeros((), jnp.bfloat16)
    for tap in range(taps):
        column = jnp.broadcast_to(local[:, tap : tap + 1], (rows, 128))
        for b, (_, start) in enumerate(blocks):
            wanted = (column - start).astype(jnp.int16)
            wanted = jnp.concatenate([wanted] * (rows // 128), axis=1)
            select_ref[tap * rows : (tap + 1) * rows, b * rows : (b + 1) * rows] = jnp.where(
                wanted == places, one, zero
            )
    for first in range(0, taps, GROUP):
        part = select_ref[first * rows : (first + GROUP) * rows]
        picked = sum(
            jnp.dot(part[:, b * rows : (b + 1) * rows], block, preferred_element_type=jnp.float32)
            for b, (block, _) in enumerate(blocks)
        ).astype(jnp.bfloat16)
        for j in range(GROUP):
            put(first + j, picked[j * rows : (j + 1) * rows])


def pick_near(local, here, partner, select_ref, near_ref):
    rows, chans = here.shape
    blocks = ((here, rows), (partner, 2 * rows * (1 - lax.axis_index("core"))))

    def put(tap, picked):
        near_ref[:, tap * chans : (tap + 1) * chans] = picked

    pick(local, near_ref.shape[1] // chans, blocks, select_ref, put)


def convolved(local, across, near_ref, weight_ref, select_ref, picked_ref):
    rows, chans = across.shape
    taps = weight_ref.shape[0]

    def put(tap, picked):
        columns = slice(tap * chans, (tap + 1) * chans)
        picked_ref[:, columns] = near_ref[:, columns] + picked

    pick(local, taps, ((across, 2 * rows * lax.axis_index("core")),), select_ref, put)
    return jnp.dot(
        picked_ref[...],
        weight_ref[...].reshape(taps * chans, weight_ref.shape[2]),
        preferred_element_type=jnp.float32,
    )


def first_near_kernel(taps_ref, here, partner, near_ref, local_ref, select_ref):
    local = local_table(taps_ref)
    local_ref[...] = local
    pick_near(local, here[...], partner[...], select_ref, near_ref)


def first_far_kernel(
    local_ref, across, near_ref, weight_ref, gain_ref, parent_ref, middle_ref, select_ref, picked_ref
):
    total = convolved(local_ref[...], across[...], near_ref, weight_ref, select_ref, picked_ref)
    rows = total.shape[0]
    middle_ref[:rows] = settled(total, gain_ref[...]).astype(middle_ref.dtype)
    ids = parent_ref[...] - lax.axis_index(SPACE) * PAR_ROWS
    ids = jnp.broadcast_to(ids.astype(jnp.float32), (middle_ref.shape[0] - rows, ids.shape[1]))
    middle_ref[rows:] = ids.astype(middle_ref.dtype)


def second_near_kernel(local_ref, here, partner, near_ref, select_ref):
    rows = local_ref.shape[0]
    pick_near(local_ref[...], here[:rows], partner[:rows], select_ref, near_ref)


def membership(ids, parents):
    return (lax.broadcasted_iota(jnp.int32, (parents, ids.shape[1]), 0) == ids).astype(jnp.float32)


def second_far_kernel(
    local_ref, across, partner, near_ref, weight_ref, gain_ref, feature_ref, parent_ref,
    cotangent_ref, after_ref,
    fine_ref, own_ref, sent_ref, grad_ref, select_ref, picked_ref,
):
    rows, chans = feature_ref.shape
    total = convolved(local_ref[...], across[:rows], near_ref, weight_ref, select_ref, picked_ref)
    fine = feature_ref[...].astype(jnp.float32) + settled(total, gain_ref[...])
    fine = fine.astype(fine_ref.dtype)
    fine_ref[...] = fine
    half = cotangent_ref.shape[0]
    member = membership(parent_ref[...] - lax.axis_index(SPACE) * half, 2 * half)
    sums = jnp.dot(member.astype(jnp.bfloat16), fine, preferred_element_type=jnp.float32)

    def tally(ids):
        return jnp.sum(membership(ids, 2 * half), axis=1, keepdims=True)

    tally_own = jnp.sum(member, axis=1, keepdims=True)
    tally_partner = tally(partner[rows:].astype(jnp.float32)[:1].astype(jnp.int32))
    tally_across = tally(across[rows:].astype(jnp.float32)[:1].astype(jnp.int32))
    upper = lax.axis_index("core") == 1
    tally_before = jnp.where(upper, tally_partner, tally_across)[half:]
    tally_after = jnp.where(upper, tally_across, tally_partner)[:half]
    count_own = jnp.maximum(tally_own[:half] + tally_before, 1.0)
    count_after = jnp.maximum(tally_own[half:] + tally_after, 1.0)
    own_ref[:, :chans] = sums[:half]
    own_ref[:, chans:] = jnp.broadcast_to(count_own, (half, own_ref.shape[1] - chans))
    sent_ref[...] = sums[half:]
    shares = sums / jnp.concatenate([count_own, count_after], axis=0)
    grads_in = jnp.concatenate([cotangent_ref[...], after_ref[...]], axis=0)
    grad_ref[...] = lax.dot_general(
        shares.astype(jnp.bfloat16), grads_in, (((0,), (0,)), ((), ())), preferred_element_type=jnp.float32
    ).astype(grad_ref.dtype)


def coarse_kernel(own_ref, moved_ref, down_ref, coarse_ref):
    chans = down_ref.shape[0]
    own = own_ref[...]
    pooled = ((own[:, :chans] + moved_ref[...]) / own[:, chans : chans + 1]).astype(jnp.bfloat16)
    coarse_ref[...] = jnp.dot(pooled, down_ref[...], preferred_element_type=jnp.float32).astype(coarse_ref.dtype)


def in_vmem(kernel, outs, inputs, name, scratch=(), flops=0):
    vmem = pl.BlockSpec(memory_space=pltpu.VMEM)
    return pl.pallas_call(
        kernel,
        out_shape=outs,
        in_specs=[vmem] * len(inputs),
        out_specs=jax.tree.map(lambda _: vmem, outs),
        scratch_shapes=scratch,
        compiler_params=pltpu.CompilerParams(vmem_limit_bytes=VMEM_BYTES),
        cost_estimate=pl.CostEstimate(flops=flops, bytes_accessed=COST_BYTES, transcendentals=0),
        name=name,
    )(*inputs)


def exchanged(pieces, axes):
    return lax.all_to_all(pieces, axes, 0, 0, tiled=True)


def plane_summed(local_grad):
    rows, cols = local_grad.shape
    plane = lax.axis_size(PLANE)
    return exchanged(local_grad.reshape(plane, rows // plane, cols), PLANE)


def finished(parts, scale):
    plane, _, cols = parts.shape
    part = jnp.sum(parts.astype(jnp.float32), axis=0)
    copies = jnp.broadcast_to(part[None], (lax.axis_size("z"),) + part.shape)
    part = jnp.sum(exchanged(copies, "z"), axis=0) * scale
    copies = jnp.broadcast_to(part.astype(jnp.bfloat16)[None], (plane,) + part.shape)
    return exchanged(copies, PLANE).astype(jnp.float32).reshape(-1, cols)


def body(
    features,
    neighbours,
    parents,
    conv_first,
    conv_second,
    gain_first,
    gain_second,
    down_weight,
    cotangent,
):
    field, grad_in = features[0], cotangent[0]
    _, taps, rows = neighbours.shape
    chans = field.shape[1]
    par_rows, out_chans = grad_in.shape
    bf16 = functools.partial(jax.ShapeDtypeStruct, dtype=jnp.bfloat16)
    f32 = functools.partial(jax.ShapeDtypeStruct, dtype=jnp.float32)
    product = 2 * taps * rows * chans * rows
    near_shape = bf16((rows, taps * chans))
    select = [pltpu.VMEM((taps * rows, 2 * rows), jnp.bfloat16)]
    select_and_picked = [
        pltpu.VMEM((taps * rows, rows), jnp.bfloat16),
        pltpu.VMEM((rows, taps * chans), jnp.bfloat16),
    ]
    across = from_across(field)
    near, local = in_vmem(
        first_near_kernel,
        (near_shape, jax.ShapeDtypeStruct((rows, taps + -taps % 8), jnp.int32)),
        (jnp.moveaxis(neighbours, 1, 0), field, from_partner(field)),
        "first_near", select, 2 * product,
    )
    ready, near = lax.optimization_barrier((grad_in, near))
    after = shifted(ready, -1)
    middle = in_vmem(
        first_far_kernel,
        bf16((rows + 16, chans)),
        (local, across, near, conv_first, gain_first[None], parents),
        "first_far", select_and_picked, 2 * product,
    )
    middle, after = lax.optimization_barrier((middle, after))
    across = from_across(middle)
    partner = from_partner(middle)
    near = in_vmem(
        second_near_kernel, near_shape, (local, middle, partner), "second_near", select, 2 * product
    )
    fine, own, sent, local_grad = in_vmem(
        second_far_kernel,
        (
            bf16((rows, chans)),
            f32((par_rows, chans + 128)),
            f32((par_rows, chans)),
            bf16((chans, out_chans)),
        ),
        (
            local, across, partner, near, conv_second, gain_second[None], field, parents,
            grad_in, after,
        ),
        "second_far", select_and_picked, 2 * product,
    )
    parts = plane_summed(local_grad)
    sent, parts = lax.optimization_barrier((sent, parts))
    coarse = in_vmem(
        coarse_kernel, bf16((par_rows, out_chans)), (own, shifted(sent, 1), down_weight), "coarse"
    )
    worlds_all = lax.axis_size(DP)
    parents_all = par_rows * lax.axis_size(SPACE)
    down_grad = finished(parts, 1.0 / math.sqrt(worlds_all * parents_all))
    return (fine[None], coarse[None], down_grad)


def solution(mesh):
    return jax.shard_map(
        body,
        mesh=split_mesh(mesh),
        in_specs=(
            P(DP, SPACE, None),
            P(DP, None, SPACE),
            P(DP, SPACE),
            P(),
            P(),
            P(),
            P(),
            P(),
            P(DP, SPACE, None),
        ),
        out_specs=(P(DP, SPACE, None), P(DP, SPACE, None), P()),
        check_vma=False,
    )
```

```python
import functools
import math

import jax
import jax.numpy as jnp
from jax import lax
from jax.experimental import pallas as pl
from jax.experimental.pallas import tpu as pltpu
from jax.sharding import Mesh
from jax.sharding import PartitionSpec as P


DP = "y"
SPACE = ("z", "x", "core")
PLANE = ("y", "x", "core")
GROUP = 3
VMEM_BYTES = 32 << 20
COST_BYTES = 1 << 20


def split_mesh(mesh):
    dp, space = mesh.devices.shape
    return Mesh(mesh.devices.reshape(dp, space // 8, 4, 2), (DP,) + SPACE)


def shifted(array, by):
    length = lax.axis_size(SPACE)
    return lax.ppermute(array, SPACE, [(i, i + by) for i in range(length) if 0 <= i + by < length])


def from_partner(array):
    length = lax.axis_size(SPACE)
    return lax.ppermute(array, SPACE, [(i, i ^ 1) for i in range(length)])


def from_across(array):
    last = lax.axis_size(SPACE) - 1
    pairs = [(i, i + 1) for i in range(1, last, 2)]
    return lax.ppermute(array, SPACE, [(0, 0), (last, last)] + pairs + [(j, i) for i, j in pairs])


def settled(running, gain):
    inverse = lax.rsqrt(jnp.mean(running * running, axis=-1, keepdims=True) + 1e-05)
    scaled = running * inverse * gain
    return scaled / (1.0 + jnp.exp(-scaled))


def local_table(taps_ref):
    taps, _, rows = taps_ref.shape
    lowest = (lax.axis_index(SPACE) - 1) * rows
    ids = taps_ref[...].reshape(taps, rows)
    local = jnp.where(ids < 0, -4 * rows, ids - lowest)
    return jnp.concatenate([local, jnp.full((-taps % 8, rows), -1, jnp.int32)], axis=0).T


def pick(local, taps, blocks, select_ref, put):
    rows = local.shape[0]
    places = lax.broadcasted_iota(jnp.int16, (rows, rows), 1)
    one, zero = jnp.ones((), jnp.bfloat16), jnp.zeros((), jnp.bfloat16)
    for tap in range(taps):
        column = jnp.broadcast_to(local[:, tap : tap + 1], (rows, 128))
        for b, (_, start) in enumerate(blocks):
            wanted = (column - start).astype(jnp.int16)
            wanted = jnp.concatenate([wanted] * (rows // 128), axis=1)
            select_ref[tap * rows : (tap + 1) * rows, b * rows : (b + 1) * rows] = jnp.where(
                wanted == places, one, zero
            )
    for first in range(0, taps, GROUP):
        part = select_ref[first * rows : (first + GROUP) * rows]
        picked = sum(
            jnp.dot(part[:, b * rows : (b + 1) * rows], block, preferred_element_type=jnp.float32)
            for b, (block, _) in enumerate(blocks)
        ).astype(jnp.bfloat16)
        for j in range(GROUP):
            put(first + j, picked[j * rows : (j + 1) * rows])


def pick_near(local, here, partner, select_ref, near_ref):
    rows, chans = here.shape
    blocks = ((here, rows), (partner, 2 * rows * (1 - lax.axis_index("core"))))

    def put(tap, picked):
        near_ref[:, tap * chans : (tap + 1) * chans] = picked

    pick(local, near_ref.shape[1] // chans, blocks, select_ref, put)


def convolved(local, across, near_ref, weight_ref, select_ref, picked_ref):
    rows, chans = across.shape
    taps = weight_ref.shape[0]

    def put(tap, picked):
        columns = slice(tap * chans, (tap + 1) * chans)
        picked_ref[:, columns] = near_ref[:, columns] + picked

    pick(local, taps, ((across, 2 * rows * lax.axis_index("core")),), select_ref, put)
    return jnp.dot(
        picked_ref[...],
        weight_ref[...].reshape(taps * chans, weight_ref.shape[2]),
        preferred_element_type=jnp.float32,
    )


def first_near_kernel(taps_ref, here, partner, near_ref, local_ref, select_ref):
    local = local_table(taps_ref)
    local_ref[...] = local
    pick_near(local, here[...], partner[...], select_ref, near_ref)


def first_far_kernel(
    local_ref, across, near_ref, weight_ref, gain_ref, parent_ref, cotangent_ref,
    middle_ref, select_ref, picked_ref,
):
    total = convolved(local_ref[...], across[...], near_ref, weight_ref, select_ref, picked_ref)
    rows = total.shape[0]
    middle_ref[:rows] = settled(total, gain_ref[...]).astype(middle_ref.dtype)
    half, wide = cotangent_ref.shape
    for j in range(wide // rows):
        middle_ref[rows + j * half : rows + (j + 1) * half] = cotangent_ref[:, j * rows : (j + 1) * rows]
    ids = parent_ref[...] - lax.axis_index(SPACE) * half
    last = rows + half * (wide // rows)
    ids = jnp.broadcast_to(ids.astype(jnp.float32), (middle_ref.shape[0] - last, ids.shape[1]))
    middle_ref[last:] = ids.astype(middle_ref.dtype)


def second_near_kernel(local_ref, here, partner, near_ref, select_ref):
    rows = local_ref.shape[0]
    pick_near(local_ref[...], here[:rows], partner[:rows], select_ref, near_ref)


def membership(ids, parents):
    return (lax.broadcasted_iota(jnp.int32, (parents, ids.shape[1]), 0) == ids).astype(jnp.float32)


def second_far_kernel(
    local_ref, across, partner, near_ref, weight_ref, gain_ref, feature_ref, parent_ref,
    cotangent_ref,
    fine_ref, own_ref, sent_ref, grad_ref, select_ref, picked_ref,
):
    rows, chans = feature_ref.shape
    total = convolved(local_ref[...], across[:rows], near_ref, weight_ref, select_ref, picked_ref)
    fine = feature_ref[...].astype(jnp.float32) + settled(total, gain_ref[...])
    fine = fine.astype(fine_ref.dtype)
    fine_ref[...] = fine
    half, wide = cotangent_ref.shape
    last = rows + half * (wide // rows)
    member = membership(parent_ref[...] - lax.axis_index(SPACE) * half, 2 * half)
    sums = jnp.dot(member.astype(jnp.bfloat16), fine, preferred_element_type=jnp.float32)

    def tally(ids):
        return jnp.sum(membership(ids, 2 * half), axis=1, keepdims=True)

    tally_own = jnp.sum(member, axis=1, keepdims=True)
    tally_partner = tally(partner[last:].astype(jnp.float32)[:1].astype(jnp.int32))
    tally_across = tally(across[last:].astype(jnp.float32)[:1].astype(jnp.int32))
    upper = lax.axis_index("core") == 1
    tally_before = jnp.where(upper, tally_partner, tally_across)[half:]
    tally_before = jnp.where(lax.axis_index(SPACE) == 0, 0.0, tally_before)
    tally_after = jnp.where(upper, tally_across, tally_partner)[:half]
    count_own = jnp.maximum(tally_own[:half] + tally_before, 1.0)
    count_after = jnp.maximum(tally_own[half:] + tally_after, 1.0)
    own_ref[:, :chans] = sums[:half]
    own_ref[:, chans:] = jnp.broadcast_to(count_own, (half, own_ref.shape[1] - chans))
    sent_ref[...] = sums[half:]
    shares = sums / jnp.concatenate([count_own, count_after], axis=0)
    after = jnp.where(upper, across[rows:last], partner[rows:last])
    after = jnp.concatenate([after[j * half : (j + 1) * half] for j in range(wide // rows)], axis=1)
    grads_in = jnp.concatenate([cotangent_ref[...], after], axis=0)
    grad_ref[...] = lax.dot_general(
        shares.astype(jnp.bfloat16), grads_in, (((0,), (0,)), ((), ())), preferred_element_type=jnp.float32
    ).astype(grad_ref.dtype)


def coarse_kernel(own_ref, moved_ref, down_ref, coarse_ref):
    chans = down_ref.shape[0]
    own = own_ref[...]
    pooled = ((own[:, :chans] + moved_ref[...]) / own[:, chans : chans + 1]).astype(jnp.bfloat16)
    coarse_ref[...] = jnp.dot(pooled, down_ref[...], preferred_element_type=jnp.float32).astype(coarse_ref.dtype)


def in_vmem(kernel, outs, inputs, name, scratch=(), flops=0):
    vmem = pl.BlockSpec(memory_space=pltpu.VMEM)
    return pl.pallas_call(
        kernel,
        out_shape=outs,
        in_specs=[vmem] * len(inputs),
        out_specs=jax.tree.map(lambda _: vmem, outs),
        scratch_shapes=scratch,
        compiler_params=pltpu.CompilerParams(vmem_limit_bytes=VMEM_BYTES),
        cost_estimate=pl.CostEstimate(flops=flops, bytes_accessed=COST_BYTES, transcendentals=0),
        name=name,
    )(*inputs)


def exchanged(pieces, axes):
    return lax.all_to_all(pieces, axes, 0, 0, tiled=True)


def plane_summed(local_grad):
    rows, cols = local_grad.shape
    plane = lax.axis_size(PLANE)
    return exchanged(local_grad.reshape(plane, rows // plane, cols), PLANE)


def finished(parts, scale):
    plane, _, cols = parts.shape
    part = jnp.sum(parts.astype(jnp.float32), axis=0)
    copies = jnp.broadcast_to(part[None], (lax.axis_size("z"),) + part.shape)
    part = jnp.sum(exchanged(copies, "z"), axis=0) * scale
    copies = jnp.broadcast_to(part.astype(jnp.bfloat16)[None], (plane,) + part.shape)
    return exchanged(copies, PLANE).astype(jnp.float32).reshape(-1, cols)


def body(
    features,
    neighbours,
    parents,
    conv_first,
    conv_second,
    gain_first,
    gain_second,
    down_weight,
    cotangent,
):
    field, grad_in = features[0], cotangent[0]
    _, taps, rows = neighbours.shape
    chans = field.shape[1]
    par_rows, out_chans = grad_in.shape
    bf16 = functools.partial(jax.ShapeDtypeStruct, dtype=jnp.bfloat16)
    f32 = functools.partial(jax.ShapeDtypeStruct, dtype=jnp.float32)
    product = 2 * taps * rows * chans * rows
    near_shape = bf16((rows, taps * chans))
    select = [pltpu.VMEM((taps * rows, 2 * rows), jnp.bfloat16)]
    select_and_picked = [
        pltpu.VMEM((taps * rows, rows), jnp.bfloat16),
        pltpu.VMEM((rows, taps * chans), jnp.bfloat16),
    ]
    across = from_across(field)
    near, local = in_vmem(
        first_near_kernel,
        (near_shape, jax.ShapeDtypeStruct((rows, taps + -taps % 8), jnp.int32)),
        (jnp.moveaxis(neighbours, 1, 0), field, from_partner(field)),
        "first_near", select, 2 * product,
    )
    middle = in_vmem(
        first_far_kernel,
        bf16((rows + par_rows * (out_chans // chans) + 16, chans)),
        (local, across, near, conv_first, gain_first[None], parents, grad_in),
        "first_far", select_and_picked, 2 * product,
    )
    across = from_across(middle)
    partner = from_partner(middle)
    near = in_vmem(
        second_near_kernel, near_shape, (local, middle, partner), "second_near", select, 2 * product
    )
    fine, own, sent, local_grad = in_vmem(
        second_far_kernel,
        (
            bf16((rows, chans)),
            f32((par_rows, chans + 128)),
            f32((par_rows, chans)),
            bf16((chans, out_chans)),
        ),
        (
            local, across, partner, near, conv_second, gain_second[None], field, parents,
            grad_in,
        ),
        "second_far", select_and_picked, 2 * product,
    )
    parts = plane_summed(local_grad)
    coarse = in_vmem(
        coarse_kernel, bf16((par_rows, out_chans)), (own, shifted(sent, 1), down_weight), "coarse"
    )
    coarse, parts = lax.optimization_barrier((coarse, parts))
    worlds_all = lax.axis_size(DP)
    parents_all = par_rows * lax.axis_size(SPACE)
    down_grad = finished(parts, 1.0 / math.sqrt(worlds_all * parents_all))
    return (fine[None], coarse[None], down_grad)


def solution(mesh):
    return jax.shard_map(
        body,
        mesh=split_mesh(mesh),
        in_specs=(
            P(DP, SPACE, None),
            P(DP, None, SPACE),
            P(DP, SPACE),
            P(),
            P(),
            P(),
            P(),
            P(),
            P(DP, SPACE, None),
        ),
        out_specs=(P(DP, SPACE, None), P(DP, SPACE, None), P()),
        check_vma=False,
    )
```

```python
import functools
import math

import jax
import jax.numpy as jnp
from jax import lax
from jax.experimental import pallas as pl
from jax.experimental.pallas import tpu as pltpu
from jax.sharding import Mesh
from jax.sharding import PartitionSpec as P


DP = "y"
SPACE = ("z", "x", "core")
PLANE = ("y", "x", "core")
GROUP = 3
VMEM_BYTES = 32 << 20
COST_BYTES = 1 << 20


def split_mesh(mesh):
    dp, space = mesh.devices.shape
    return Mesh(mesh.devices.reshape(dp, space // 8, 4, 2), (DP,) + SPACE)


def shifted(array, by):
    length = lax.axis_size(SPACE)
    return lax.ppermute(array, SPACE, [(i, (i + by) % length) for i in range(length)])


def from_partner(array):
    length = lax.axis_size(SPACE)
    return lax.ppermute(array, SPACE, [(i, i ^ 1) for i in range(length)])


def settled(running, gain):
    inverse = lax.rsqrt(jnp.mean(running * running, axis=-1, keepdims=True) + 1e-05)
    scaled = running * inverse * gain
    return scaled / (1.0 + jnp.exp(-scaled))


def local_table(taps_ref):
    taps, _, rows = taps_ref.shape
    lowest = (lax.axis_index(SPACE) - 1) * rows
    ids = taps_ref[...].reshape(taps, rows)
    local = jnp.where(ids < 0, -4 * rows, ids - lowest)
    return jnp.concatenate([local, jnp.full((-taps % 8, rows), -1, jnp.int32)], axis=0).T


def pick(local, taps, blocks, select_ref, put):
    rows = local.shape[0]
    places = lax.broadcasted_iota(jnp.int16, (rows, rows), 1)
    one, zero = jnp.ones((), jnp.bfloat16), jnp.zeros((), jnp.bfloat16)
    for tap in range(taps):
        column = jnp.broadcast_to(local[:, tap : tap + 1], (rows, 128))
        for b, (_, start) in enumerate(blocks):
            wanted = (column - start).astype(jnp.int16)
            wanted = jnp.concatenate([wanted] * (rows // 128), axis=1)
            select_ref[tap * rows : (tap + 1) * rows, b * rows : (b + 1) * rows] = jnp.where(
                wanted == places, one, zero
            )
    for first in range(0, taps, GROUP):
        part = select_ref[first * rows : (first + GROUP) * rows]
        picked = sum(
            jnp.dot(part[:, b * rows : (b + 1) * rows], block, preferred_element_type=jnp.float32)
            for b, (block, _) in enumerate(blocks)
        ).astype(jnp.bfloat16)
        for j in range(GROUP):
            put(first + j, picked[j * rows : (j + 1) * rows])


def pick_near(local, here, partner, select_ref, near_ref):
    rows, chans = here.shape
    blocks = ((here, rows), (partner, 2 * rows * (1 - lax.axis_index("core"))))

    def put(tap, picked):
        near_ref[:, tap * chans : (tap + 1) * chans] = picked

    pick(local, near_ref.shape[1] // chans, blocks, select_ref, put)


def convolved(local, before, after, near_ref, weight_ref, select_ref, picked_ref):
    rows, chans = before.shape
    across = jnp.where(lax.axis_index("core") == 1, after, before)
    taps = weight_ref.shape[0]

    def put(tap, picked):
        columns = slice(tap * chans, (tap + 1) * chans)
        picked_ref[:, columns] = near_ref[:, columns] + picked

    pick(local, taps, ((across, 2 * rows * lax.axis_index("core")),), select_ref, put)
    return jnp.dot(
        picked_ref[...],
        weight_ref[...].reshape(taps * chans, weight_ref.shape[2]),
        preferred_element_type=jnp.float32,
    )


def first_near_kernel(taps_ref, here, partner, near_ref, local_ref, select_ref):
    local = local_table(taps_ref)
    local_ref[...] = local
    pick_near(local, here[...], partner[...], select_ref, near_ref)


def first_far_kernel(
    local_ref, before, after, near_ref, weight_ref, gain_ref, parent_ref, cotangent_ref,
    middle_ref, wide_ref, select_ref, picked_ref,
):
    total = convolved(local_ref[...], before[...], after[...], near_ref, weight_ref, select_ref, picked_ref)
    rows = total.shape[0]
    middle = settled(total, gain_ref[...]).astype(middle_ref.dtype)
    middle_ref[:rows] = middle
    wide_ref[:rows] = middle
    half, wide = cotangent_ref.shape
    for j in range(wide // rows):
        wide_ref[rows + j * half : rows + (j + 1) * half] = cotangent_ref[:, j * rows : (j + 1) * rows]
    ids = parent_ref[...] - lax.axis_index(SPACE) * half
    ids = jnp.broadcast_to(ids.astype(jnp.float32), (middle_ref.shape[0] - rows, ids.shape[1]))
    middle_ref[rows:] = ids.astype(middle_ref.dtype)
    wide_ref[rows + half * (wide // rows) :] = ids.astype(wide_ref.dtype)


def second_near_kernel(local_ref, here, partner, near_ref, select_ref):
    rows = local_ref.shape[0]
    pick_near(local_ref[...], here[:rows], partner[:rows], select_ref, near_ref)


def membership(ids, parents):
    return (lax.broadcasted_iota(jnp.int32, (parents, ids.shape[1]), 0) == ids).astype(jnp.float32)


def second_far_kernel(
    local_ref, before, after, near_ref, weight_ref, gain_ref, feature_ref, parent_ref,
    cotangent_ref,
    fine_ref, own_ref, sent_ref, grad_ref, select_ref, picked_ref,
):
    rows, chans = feature_ref.shape
    total = convolved(local_ref[...], before[:rows], after[:rows], near_ref, weight_ref, select_ref, picked_ref)
    fine = feature_ref[...].astype(jnp.float32) + settled(total, gain_ref[...])
    fine = fine.astype(fine_ref.dtype)
    fine_ref[...] = fine
    half, wide = cotangent_ref.shape
    last = rows + half * (wide // rows)
    member = membership(parent_ref[...] - lax.axis_index(SPACE) * half, 2 * half)
    sums = jnp.dot(member.astype(jnp.bfloat16), fine, preferred_element_type=jnp.float32)

    def tally(ids):
        return jnp.sum(membership(ids, 2 * half), axis=1, keepdims=True)

    tally_own = jnp.sum(member, axis=1, keepdims=True)
    tally_before = tally(before[rows:].astype(jnp.float32)[:1].astype(jnp.int32))[half:]
    tally_after = tally(after[last:].astype(jnp.float32)[:1].astype(jnp.int32))[:half]
    count_own = jnp.maximum(tally_own[:half] + tally_before, 1.0)
    count_after = jnp.maximum(tally_own[half:] + tally_after, 1.0)
    own_ref[:, :chans] = sums[:half]
    own_ref[:, chans:] = jnp.broadcast_to(count_own, (half, own_ref.shape[1] - chans))
    sent_ref[...] = sums[half:]
    shares = sums / jnp.concatenate([count_own, count_after], axis=0)
    next_grads = after[rows:last]
    next_grads = jnp.concatenate([next_grads[j * half : (j + 1) * half] for j in range(wide // rows)], axis=1)
    grads_in = jnp.concatenate([cotangent_ref[...], next_grads], axis=0)
    grad_ref[...] = lax.dot_general(
        shares.astype(jnp.bfloat16), grads_in, (((0,), (0,)), ((), ())), preferred_element_type=jnp.float32
    ).astype(grad_ref.dtype)


def coarse_kernel(own_ref, moved_ref, down_ref, coarse_ref):
    chans = down_ref.shape[0]
    own = own_ref[...]
    pooled = ((own[:, :chans] + moved_ref[...]) / own[:, chans : chans + 1]).astype(jnp.bfloat16)
    coarse_ref[...] = jnp.dot(pooled, down_ref[...], preferred_element_type=jnp.float32).astype(coarse_ref.dtype)


def in_vmem(kernel, outs, inputs, name, scratch=(), flops=0):
    vmem = pl.BlockSpec(memory_space=pltpu.VMEM)
    return pl.pallas_call(
        kernel,
        out_shape=outs,
        in_specs=[vmem] * len(inputs),
        out_specs=jax.tree.map(lambda _: vmem, outs),
        scratch_shapes=scratch,
        compiler_params=pltpu.CompilerParams(vmem_limit_bytes=VMEM_BYTES),
        cost_estimate=pl.CostEstimate(flops=flops, bytes_accessed=COST_BYTES, transcendentals=0),
        name=name,
    )(*inputs)


def exchanged(pieces, axes):
    return lax.all_to_all(pieces, axes, 0, 0, tiled=True)


def plane_summed(local_grad):
    rows, cols = local_grad.shape
    plane = lax.axis_size(PLANE)
    return exchanged(local_grad.reshape(plane, rows // plane, cols), PLANE)


def finished(parts, scale):
    plane, _, cols = parts.shape
    part = jnp.sum(parts.astype(jnp.float32), axis=0)
    copies = jnp.broadcast_to(part[None], (lax.axis_size("z"),) + part.shape)
    part = jnp.sum(exchanged(copies, "z"), axis=0) * scale
    copies = jnp.broadcast_to(part.astype(jnp.bfloat16)[None], (plane,) + part.shape)
    return exchanged(copies, PLANE).astype(jnp.float32).reshape(-1, cols)


def body(
    features,
    neighbours,
    parents,
    conv_first,
    conv_second,
    gain_first,
    gain_second,
    down_weight,
    cotangent,
):
    field, grad_in = features[0], cotangent[0]
    _, taps, rows = neighbours.shape
    chans = field.shape[1]
    par_rows, out_chans = grad_in.shape
    bf16 = functools.partial(jax.ShapeDtypeStruct, dtype=jnp.bfloat16)
    f32 = functools.partial(jax.ShapeDtypeStruct, dtype=jnp.float32)
    product = 2 * taps * rows * chans * rows
    near_shape = bf16((rows, taps * chans))
    select = [pltpu.VMEM((taps * rows, 2 * rows), jnp.bfloat16)]
    select_and_picked = [
        pltpu.VMEM((taps * rows, rows), jnp.bfloat16),
        pltpu.VMEM((rows, taps * chans), jnp.bfloat16),
    ]
    before, after = shifted(field, 1), shifted(field, -1)
    near, local = in_vmem(
        first_near_kernel,
        (near_shape, jax.ShapeDtypeStruct((rows, taps + -taps % 8), jnp.int32)),
        (jnp.moveaxis(neighbours, 1, 0), field, from_partner(field)),
        "first_near", select, 2 * product,
    )
    middle, wide = in_vmem(
        first_far_kernel,
        (bf16((rows + 16, chans)), bf16((rows + par_rows * (out_chans // chans) + 16, chans))),
        (local, before, after, near, conv_first, gain_first[None], parents, grad_in),
        "first_far", select_and_picked, 2 * product,
    )
    before, after = shifted(middle, 1), shifted(wide, -1)
    partner = from_partner(middle)
    near = in_vmem(
        second_near_kernel, near_shape, (local, middle, partner), "second_near", select, 2 * product
    )
    fine, own, sent, local_grad = in_vmem(
        second_far_kernel,
        (
            bf16((rows, chans)),
            f32((par_rows, chans + 128)),
            f32((par_rows, chans)),
            bf16((chans, out_chans)),
        ),
        (
            local, before, after, near, conv_second, gain_second[None], field, parents,
            grad_in,
        ),
        "second_far", select_and_picked, 2 * product,
    )
    parts = plane_summed(local_grad)
    moved, parts = lax.optimization_barrier((shifted(sent, 1), parts))
    coarse = in_vmem(coarse_kernel, bf16((par_rows, out_chans)), (own, moved, down_weight), "coarse")
    worlds_all = lax.axis_size(DP)
    parents_all = par_rows * lax.axis_size(SPACE)
    down_grad = finished(parts, 1.0 / math.sqrt(worlds_all * parents_all))
    return (fine[None], coarse[None], down_grad)


def solution(mesh):
    return jax.shard_map(
        body,
        mesh=split_mesh(mesh),
        in_specs=(
            P(DP, SPACE, None),
            P(DP, None, SPACE),
            P(DP, SPACE),
            P(),
            P(),
            P(),
            P(),
            P(),
            P(DP, SPACE, None),
        ),
        out_specs=(P(DP, SPACE, None), P(DP, SPACE, None), P()),
        check_vma=False,
    )
```

```python
import functools
import math

import jax
import jax.numpy as jnp
from jax import lax
from jax.experimental import pallas as pl
from jax.experimental.pallas import tpu as pltpu
from jax.sharding import Mesh
from jax.sharding import PartitionSpec as P


DP = "y"
SPACE = ("z", "x", "core")
PLANE = ("y", "x", "core")
GROUP = 3
VMEM_BYTES = 32 << 20
COST_BYTES = 1 << 20


def split_mesh(mesh):
    dp, space = mesh.devices.shape
    return Mesh(mesh.devices.reshape(dp, space // 8, 4, 2), (DP,) + SPACE)


def shifted(array, by):
    length = lax.axis_size(SPACE)
    return lax.ppermute(array, SPACE, [(i, (i + by) % length) for i in range(length)])


def from_partner(array):
    length = lax.axis_size(SPACE)
    return lax.ppermute(array, SPACE, [(i, i ^ 1) for i in range(length)])


def settled(running, gain):
    inverse = lax.rsqrt(jnp.mean(running * running, axis=-1, keepdims=True) + 1e-05)
    scaled = running * inverse * gain
    return scaled / (1.0 + jnp.exp(-scaled))


def local_table(taps_ref):
    taps, _, rows = taps_ref.shape
    lowest = (lax.axis_index(SPACE) - 1) * rows
    ids = taps_ref[...].reshape(taps, rows)
    local = jnp.where(ids < 0, -4 * rows, ids - lowest)
    return jnp.concatenate([local, jnp.full((-taps % 8, rows), -1, jnp.int32)], axis=0).T


def pick(local, taps, blocks, select_ref, put, wait=None):
    rows = local.shape[0]
    places = lax.broadcasted_iota(jnp.int16, (rows, rows), 1)
    one, zero = jnp.ones((), jnp.bfloat16), jnp.zeros((), jnp.bfloat16)
    for tap in range(taps):
        column = jnp.broadcast_to(local[:, tap : tap + 1], (rows, 128))
        for b, (_, start) in enumerate(blocks):
            wanted = (column - start).astype(jnp.int16)
            wanted = jnp.concatenate([wanted] * (rows // 128), axis=1)
            select_ref[tap * rows : (tap + 1) * rows, b * rows : (b + 1) * rows] = jnp.where(
                wanted == places, one, zero
            )
    if wait is not None:
        wait()
    for first in range(0, taps, GROUP):
        part = select_ref[first * rows : (first + GROUP) * rows]
        picked = sum(
            jnp.dot(part[:, b * rows : (b + 1) * rows], block[...], preferred_element_type=jnp.float32)
            for b, (block, _) in enumerate(blocks)
        ).astype(jnp.bfloat16)
        for j in range(GROUP):
            put(first + j, picked[j * rows : (j + 1) * rows])


def pick_near(local, here, partner, select_ref, near_ref, wait=None):
    rows, chans = here.shape
    blocks = ((here, rows), (partner, 2 * rows * (1 - lax.axis_index("core"))))

    def put(tap, picked):
        near_ref[:, tap * chans : (tap + 1) * chans] = picked

    pick(local, near_ref.shape[1] // chans, blocks, select_ref, put, wait)


def convolved(local, before, after, near_ref, weight_ref, select_ref, picked_ref):
    rows, chans = before.shape
    across = jnp.where(lax.axis_index("core") == 1, after, before)
    taps = weight_ref.shape[0]

    def put(tap, picked):
        columns = slice(tap * chans, (tap + 1) * chans)
        picked_ref[:, columns] = near_ref[:, columns] + picked

    pick(local, taps, ((across, 2 * rows * lax.axis_index("core")),), select_ref, put)
    return jnp.dot(
        picked_ref[...],
        weight_ref[...].reshape(taps * chans, weight_ref.shape[2]),
        preferred_element_type=jnp.float32,
    )


def first_near_kernel(
    partner, taps_hbm, here_hbm, near_ref, local_ref, select_ref, taps_ref, here, taps_sem, here_sem
):
    taps_copy = pltpu.make_async_copy(taps_hbm, taps_ref, taps_sem)
    here_copy = pltpu.make_async_copy(here_hbm, here, here_sem)
    taps_copy.start()
    here_copy.start()
    taps_copy.wait()
    local = local_table(taps_ref)
    local_ref[...] = local
    pick_near(local, here, partner, select_ref, near_ref, here_copy.wait)


def first_far_kernel(
    local_ref, after, before, near_ref, weight_ref, gain_ref, parent_ref, cotangent_ref,
    middle_ref, wide_ref, select_ref, picked_ref,
):
    total = convolved(local_ref[...], before[...], after[...], near_ref, weight_ref, select_ref, picked_ref)
    rows = total.shape[0]
    middle = settled(total, gain_ref[...]).astype(middle_ref.dtype)
    middle_ref[:rows] = middle
    wide_ref[:rows] = middle
    half, wide = cotangent_ref.shape
    for j in range(wide // rows):
        wide_ref[rows + j * half : rows + (j + 1) * half] = cotangent_ref[:, j * rows : (j + 1) * rows]
    ids = parent_ref[...] - lax.axis_index(SPACE) * half
    ids = jnp.broadcast_to(ids.astype(jnp.float32), (middle_ref.shape[0] - rows, ids.shape[1]))
    middle_ref[rows:] = ids.astype(middle_ref.dtype)
    wide_ref[rows + half * (wide // rows) :] = ids.astype(wide_ref.dtype)


def second_near_kernel(local_ref, here, partner, near_ref, select_ref):
    rows = local_ref.shape[0]
    pick_near(local_ref[...], here[:rows], partner[:rows], select_ref, near_ref)


def membership(ids, parents):
    return (lax.broadcasted_iota(jnp.int32, (parents, ids.shape[1]), 0) == ids).astype(jnp.float32)


def second_far_kernel(
    local_ref, after, before, near_ref, weight_ref, gain_ref, feature_ref, parent_ref,
    cotangent_ref,
    fine_ref, own_ref, sent_ref, grad_ref, select_ref, picked_ref,
):
    rows, chans = feature_ref.shape
    total = convolved(local_ref[...], before[:rows], after[:rows], near_ref, weight_ref, select_ref, picked_ref)
    fine = feature_ref[...].astype(jnp.float32) + settled(total, gain_ref[...])
    fine = fine.astype(fine_ref.dtype)
    fine_ref[...] = fine
    half, wide = cotangent_ref.shape
    last = rows + half * (wide // rows)
    member = membership(parent_ref[...] - lax.axis_index(SPACE) * half, 2 * half)
    sums = jnp.dot(member.astype(jnp.bfloat16), fine, preferred_element_type=jnp.float32)

    def tally(ids):
        return jnp.sum(membership(ids, 2 * half), axis=1, keepdims=True)

    tally_own = jnp.sum(member, axis=1, keepdims=True)
    tally_before = tally(before[last:].astype(jnp.float32)[:1].astype(jnp.int32))[half:]
    tally_after = tally(after[last:].astype(jnp.float32)[:1].astype(jnp.int32))[:half]
    count_own = jnp.maximum(tally_own[:half] + tally_before, 1.0)
    count_after = jnp.maximum(tally_own[half:] + tally_after, 1.0)
    own_ref[:, :chans] = sums[:half]
    own_ref[:, chans:] = jnp.broadcast_to(count_own, (half, own_ref.shape[1] - chans))
    sent_ref[...] = sums[half:]
    shares = sums / jnp.concatenate([count_own, count_after], axis=0)
    next_grads = after[rows:last]
    next_grads = jnp.concatenate([next_grads[j * half : (j + 1) * half] for j in range(wide // rows)], axis=1)
    grads_in = jnp.concatenate([cotangent_ref[...], next_grads], axis=0)
    grad_ref[...] = lax.dot_general(
        shares.astype(jnp.bfloat16), grads_in, (((0,), (0,)), ((), ())), preferred_element_type=jnp.float32
    ).astype(grad_ref.dtype)


def coarse_kernel(own_ref, moved_ref, down_ref, coarse_ref):
    chans = down_ref.shape[0]
    own = own_ref[...]
    pooled = ((own[:, :chans] + moved_ref[...]) / own[:, chans : chans + 1]).astype(jnp.bfloat16)
    coarse_ref[...] = jnp.dot(pooled, down_ref[...], preferred_element_type=jnp.float32).astype(coarse_ref.dtype)


def in_vmem(kernel, outs, inputs, name, scratch=(), flops=0, from_hbm=()):
    vmem = pl.BlockSpec(memory_space=pltpu.VMEM)
    return pl.pallas_call(
        kernel,
        out_shape=outs,
        in_specs=[vmem] * len(inputs) + [pl.BlockSpec(memory_space=pltpu.HBM)] * len(from_hbm),
        out_specs=jax.tree.map(lambda _: vmem, outs),
        scratch_shapes=scratch,
        compiler_params=pltpu.CompilerParams(vmem_limit_bytes=VMEM_BYTES),
        cost_estimate=pl.CostEstimate(flops=flops, bytes_accessed=COST_BYTES, transcendentals=0),
        name=name,
    )(*inputs, *[pltpu.with_memory_space_constraint(array, pltpu.HBM) for array in from_hbm])


def exchanged(pieces, axes):
    return lax.all_to_all(pieces, axes, 0, 0, tiled=True)


def plane_summed(local_grad):
    rows, cols = local_grad.shape
    plane = lax.axis_size(PLANE)
    return exchanged(local_grad.reshape(plane, rows // plane, cols), PLANE)


def finished(parts, sent, scale):
    plane, _, cols = parts.shape
    part = jnp.sum(parts.astype(jnp.float32), axis=0)
    copies = jnp.broadcast_to(part[None], (lax.axis_size("z"),) + part.shape)
    moved, copies = lax.optimization_barrier((shifted(sent, 1), exchanged(copies, "z")))
    part = jnp.sum(copies, axis=0) * scale
    copies = jnp.broadcast_to(part.astype(jnp.bfloat16)[None], (plane,) + part.shape)
    return exchanged(copies, PLANE).astype(jnp.float32).reshape(-1, cols), moved


def body(
    features,
    neighbours,
    parents,
    conv_first,
    conv_second,
    gain_first,
    gain_second,
    down_weight,
    cotangent,
):
    field, grad_in = features[0], cotangent[0]
    _, taps, rows = neighbours.shape
    chans = field.shape[1]
    par_rows, out_chans = grad_in.shape
    bf16 = functools.partial(jax.ShapeDtypeStruct, dtype=jnp.bfloat16)
    f32 = functools.partial(jax.ShapeDtypeStruct, dtype=jnp.float32)
    product = 2 * taps * rows * chans * rows
    near_shape = bf16((rows, taps * chans))
    select = [pltpu.VMEM((taps * rows, 2 * rows), jnp.bfloat16)]
    select_and_picked = [
        pltpu.VMEM((taps * rows, rows), jnp.bfloat16),
        pltpu.VMEM((rows, taps * chans), jnp.bfloat16),
    ]
    after, before = shifted(field, -1), shifted(field, 1)
    near, local = in_vmem(
        first_near_kernel,
        (near_shape, jax.ShapeDtypeStruct((rows, taps + -taps % 8), jnp.int32)),
        (from_partner(field),),
        "first_near",
        select
        + [
            pltpu.VMEM((taps, 1, rows), jnp.int32),
            pltpu.VMEM((rows, chans), jnp.bfloat16),
            pltpu.SemaphoreType.DMA,
            pltpu.SemaphoreType.DMA,
        ],
        2 * product,
        (jnp.moveaxis(neighbours, 1, 0), field),
    )
    middle, wide = in_vmem(
        first_far_kernel,
        (bf16((rows + 16, chans)), bf16((rows + par_rows * (out_chans // chans) + 16, chans))),
        (local, after, before, near, conv_first, gain_first[None], parents, grad_in),
        "first_far", select_and_picked, 2 * product,
    )
    after, before = shifted(wide, -1), shifted(wide, 1)
    partner = from_partner(middle)
    near = in_vmem(
        second_near_kernel, near_shape, (local, middle, partner), "second_near", select, 2 * product
    )
    fine, own, sent, local_grad = in_vmem(
        second_far_kernel,
        (
            bf16((rows, chans)),
            f32((par_rows, chans + 128)),
            f32((par_rows, chans)),
            bf16((chans, out_chans)),
        ),
        (
            local, after, before, near, conv_second, gain_second[None], field, parents,
            grad_in,
        ),
        "second_far", select_and_picked, 2 * product,
    )
    parts = plane_summed(local_grad)
    worlds_all = lax.axis_size(DP)
    parents_all = par_rows * lax.axis_size(SPACE)
    down_grad, moved = finished(parts, sent, 1.0 / math.sqrt(worlds_all * parents_all))
    coarse = in_vmem(coarse_kernel, bf16((par_rows, out_chans)), (own, moved, down_weight), "coarse")
    return (fine[None], coarse[None], down_grad)


def solution(mesh):
    return jax.shard_map(
        body,
        mesh=split_mesh(mesh),
        in_specs=(
            P(DP, SPACE, None),
            P(DP, None, SPACE),
            P(DP, SPACE),
            P(),
            P(),
            P(),
            P(),
            P(),
            P(DP, SPACE, None),
        ),
        out_specs=(P(DP, SPACE, None), P(DP, SPACE, None), P()),
        check_vma=False,
    )
```

```python
import functools
import math

import jax
import jax.numpy as jnp
from jax import lax
from jax.experimental import pallas as pl
from jax.experimental.pallas import tpu as pltpu
from jax.sharding import Mesh
from jax.sharding import PartitionSpec as P


DP = "y"
SPACE = ("z", "x", "core")
PLANE = ("y", "x", "core")
GROUP = 3
VMEM_BYTES = 32 << 20
PAR_ROWS = 64
COST_BYTES = 1 << 20


def split_mesh(mesh):
    dp, space = mesh.devices.shape
    return Mesh(mesh.devices.reshape(dp, space // 8, 4, 2), (DP,) + SPACE)


def shifted(array, by):
    length = lax.axis_size(SPACE)
    return lax.ppermute(array, SPACE, [(i, (i + by) % length) for i in range(length)])


def from_partner(array):
    length = lax.axis_size(SPACE)
    return lax.ppermute(array, SPACE, [(i, i ^ 1) for i in range(length)])


def settled(running, gain):
    inverse = lax.rsqrt(jnp.mean(running * running, axis=-1, keepdims=True) + 1e-05)
    scaled = running * inverse * gain
    return scaled / (1.0 + jnp.exp(-scaled))


def local_table(taps_ref):
    taps, _, rows = taps_ref.shape
    lowest = (lax.axis_index(SPACE) - 1) * rows
    ids = taps_ref[...].reshape(taps, rows)
    local = jnp.where(ids < 0, -4 * rows, ids - lowest)
    return jnp.concatenate([local, jnp.full((-taps % 8, rows), -1, jnp.int32)], axis=0).T


def pick(local, taps, blocks, select_ref, put, wait=None):
    rows = local.shape[0]
    places = lax.broadcasted_iota(jnp.int16, (rows, rows), 1)
    one, zero = jnp.ones((), jnp.bfloat16), jnp.zeros((), jnp.bfloat16)
    for tap in range(taps):
        column = jnp.broadcast_to(local[:, tap : tap + 1], (rows, 128))
        for b, (_, start) in enumerate(blocks):
            wanted = (column - start).astype(jnp.int16)
            wanted = jnp.concatenate([wanted] * (rows // 128), axis=1)
            select_ref[tap * rows : (tap + 1) * rows, b * rows : (b + 1) * rows] = jnp.where(
                wanted == places, one, zero
            )
    if wait is not None:
        wait()
    for first in range(0, taps, GROUP):
        part = select_ref[first * rows : (first + GROUP) * rows]
        picked = sum(
            jnp.dot(part[:, b * rows : (b + 1) * rows], block[...], preferred_element_type=jnp.float32)
            for b, (block, _) in enumerate(blocks)
        ).astype(jnp.bfloat16)
        for j in range(GROUP):
            put(first + j, picked[j * rows : (j + 1) * rows])


def pick_near(local, here, partner, select_ref, near_ref, wait=None):
    rows, chans = here.shape
    blocks = ((here, rows), (partner, 2 * rows * (1 - lax.axis_index("core"))))

    def put(tap, picked):
        near_ref[:, tap * chans : (tap + 1) * chans] = picked

    pick(local, near_ref.shape[1] // chans, blocks, select_ref, put, wait)


def convolved(local, before, after, near_ref, weight_ref, select_ref, picked_ref):
    rows, chans = before.shape
    across = jnp.where(lax.axis_index("core") == 1, after, before)
    taps = weight_ref.shape[0]

    def put(tap, picked):
        columns = slice(tap * chans, (tap + 1) * chans)
        picked_ref[:, columns] = near_ref[:, columns] + picked

    pick(local, taps, ((across, 2 * rows * lax.axis_index("core")),), select_ref, put)
    return jnp.dot(
        picked_ref[...],
        weight_ref[...].reshape(taps * chans, weight_ref.shape[2]),
        preferred_element_type=jnp.float32,
    )


def first_near_kernel(
    partner, taps_hbm, here_hbm, near_ref, local_ref, select_ref, taps_ref, here, taps_sem, here_sem
):
    taps_copy = pltpu.make_async_copy(taps_hbm, taps_ref, taps_sem)
    here_copy = pltpu.make_async_copy(here_hbm, here, here_sem)
    taps_copy.start()
    here_copy.start()
    taps_copy.wait()
    local = local_table(taps_ref)
    local_ref[...] = local
    pick_near(local, here, partner, select_ref, near_ref, here_copy.wait)


def first_far_kernel(
    local_ref, after, before, near_ref, weight_ref, gain_ref, parent_ref,
    middle_ref, select_ref, picked_ref,
):
    total = convolved(local_ref[...], before[...], after[...], near_ref, weight_ref, select_ref, picked_ref)
    rows = total.shape[0]
    middle_ref[:rows] = settled(total, gain_ref[...]).astype(middle_ref.dtype)
    ids = parent_ref[...] - lax.axis_index(SPACE) * PAR_ROWS
    ids = jnp.broadcast_to(ids.astype(jnp.float32), (middle_ref.shape[0] - rows, ids.shape[1]))
    middle_ref[rows:] = ids.astype(middle_ref.dtype)


def second_near_kernel(local_ref, here, partner, near_ref, select_ref):
    rows = local_ref.shape[0]
    pick_near(local_ref[...], here[:rows], partner[:rows], select_ref, near_ref)


def membership(ids, parents):
    return (lax.broadcasted_iota(jnp.int32, (parents, ids.shape[1]), 0) == ids).astype(jnp.float32)


def second_far_kernel(
    local_ref, after, before, near_ref, weight_ref, gain_ref, feature_ref, parent_ref,
    cotangent_ref, next_ref,
    fine_ref, own_ref, sent_ref, grad_ref, select_ref, picked_ref,
):
    rows, chans = feature_ref.shape
    total = convolved(local_ref[...], before[:rows], after[:rows], near_ref, weight_ref, select_ref, picked_ref)
    fine = feature_ref[...].astype(jnp.float32) + settled(total, gain_ref[...])
    fine = fine.astype(fine_ref.dtype)
    fine_ref[...] = fine
    half = cotangent_ref.shape[0]
    member = membership(parent_ref[...] - lax.axis_index(SPACE) * half, 2 * half)
    sums = jnp.dot(member.astype(jnp.bfloat16), fine, preferred_element_type=jnp.float32)

    def tally(ids):
        return jnp.sum(membership(ids, 2 * half), axis=1, keepdims=True)

    tally_own = jnp.sum(member, axis=1, keepdims=True)
    tally_before = tally(before[rows:].astype(jnp.float32)[:1].astype(jnp.int32))[half:]
    tally_after = tally(after[rows:].astype(jnp.float32)[:1].astype(jnp.int32))[:half]
    count_own = jnp.maximum(tally_own[:half] + tally_before, 1.0)
    count_after = jnp.maximum(tally_own[half:] + tally_after, 1.0)
    own_ref[:, :chans] = sums[:half]
    own_ref[:, chans:] = jnp.broadcast_to(count_own, (half, own_ref.shape[1] - chans))
    sent_ref[...] = sums[half:]
    shares = sums / jnp.concatenate([count_own, count_after], axis=0)
    grads_in = jnp.concatenate([cotangent_ref[...], next_ref[...]], axis=0)
    grad_ref[...] = lax.dot_general(
        shares.astype(jnp.bfloat16), grads_in, (((0,), (0,)), ((), ())), preferred_element_type=jnp.float32
    ).astype(grad_ref.dtype)


def coarse_kernel(own_ref, moved_ref, down_ref, coarse_ref):
    chans = down_ref.shape[0]
    own = own_ref[...]
    pooled = ((own[:, :chans] + moved_ref[...]) / own[:, chans : chans + 1]).astype(jnp.bfloat16)
    coarse_ref[...] = jnp.dot(pooled, down_ref[...], preferred_element_type=jnp.float32).astype(coarse_ref.dtype)


def in_vmem(kernel, outs, inputs, name, scratch=(), flops=0, from_hbm=()):
    vmem = pl.BlockSpec(memory_space=pltpu.VMEM)
    return pl.pallas_call(
        kernel,
        out_shape=outs,
        in_specs=[vmem] * len(inputs) + [pl.BlockSpec(memory_space=pltpu.HBM)] * len(from_hbm),
        out_specs=jax.tree.map(lambda _: vmem, outs),
        scratch_shapes=scratch,
        compiler_params=pltpu.CompilerParams(vmem_limit_bytes=VMEM_BYTES),
        cost_estimate=pl.CostEstimate(flops=flops, bytes_accessed=COST_BYTES, transcendentals=0),
        name=name,
    )(*inputs, *[pltpu.with_memory_space_constraint(array, pltpu.HBM) for array in from_hbm])


def exchanged(pieces, axes):
    return lax.all_to_all(pieces, axes, 0, 0, tiled=True)


def plane_summed(local_grad):
    rows, cols = local_grad.shape
    plane = lax.axis_size(PLANE)
    return exchanged(local_grad.reshape(plane, rows // plane, cols), PLANE)


def finished(parts, scale):
    plane, _, cols = parts.shape
    part = jnp.sum(parts.astype(jnp.float32), axis=0)
    copies = jnp.broadcast_to(part[None], (lax.axis_size("z"),) + part.shape)
    part = jnp.sum(exchanged(copies, "z"), axis=0) * scale
    copies = jnp.broadcast_to(part.astype(jnp.bfloat16)[None], (plane,) + part.shape)
    return exchanged(copies, PLANE).astype(jnp.float32).reshape(-1, cols)


def body(
    features,
    neighbours,
    parents,
    conv_first,
    conv_second,
    gain_first,
    gain_second,
    down_weight,
    cotangent,
):
    field, grad_in = features[0], cotangent[0]
    _, taps, rows = neighbours.shape
    chans = field.shape[1]
    par_rows, out_chans = grad_in.shape
    bf16 = functools.partial(jax.ShapeDtypeStruct, dtype=jnp.bfloat16)
    f32 = functools.partial(jax.ShapeDtypeStruct, dtype=jnp.float32)
    product = 2 * taps * rows * chans * rows
    near_shape = bf16((rows, taps * chans))
    select = [pltpu.VMEM((taps * rows, 2 * rows), jnp.bfloat16)]
    select_and_picked = [
        pltpu.VMEM((taps * rows, rows), jnp.bfloat16),
        pltpu.VMEM((rows, taps * chans), jnp.bfloat16),
    ]
    after, before = shifted(field, -1), shifted(field, 1)
    near, local = in_vmem(
        first_near_kernel,
        (near_shape, jax.ShapeDtypeStruct((rows, taps + -taps % 8), jnp.int32)),
        (from_partner(field),),
        "first_near",
        select
        + [
            pltpu.VMEM((taps, 1, rows), jnp.int32),
            pltpu.VMEM((rows, chans), jnp.bfloat16),
            pltpu.SemaphoreType.DMA,
            pltpu.SemaphoreType.DMA,
        ],
        2 * product,
        (jnp.moveaxis(neighbours, 1, 0), field),
    )
    ready, near = lax.optimization_barrier((grad_in, near))
    next_grad = shifted(ready, -1)
    middle = in_vmem(
        first_far_kernel,
        bf16((rows + 16, chans)),
        (local, after, before, near, conv_first, gain_first[None], parents),
        "first_far", select_and_picked, 2 * product,
    )
    middle, next_grad = lax.optimization_barrier((middle, next_grad))
    after, before = shifted(middle, -1), shifted(middle, 1)
    partner = from_partner(middle)
    near = in_vmem(
        second_near_kernel, near_shape, (local, middle, partner), "second_near", select, 2 * product
    )
    fine, own, sent, local_grad = in_vmem(
        second_far_kernel,
        (
            bf16((rows, chans)),
            f32((par_rows, chans + 128)),
            f32((par_rows, chans)),
            bf16((chans, out_chans)),
        ),
        (
            local, after, before, near, conv_second, gain_second[None], field, parents,
            grad_in, next_grad,
        ),
        "second_far", select_and_picked, 2 * product,
    )
    parts = plane_summed(local_grad)
    worlds_all = lax.axis_size(DP)
    parents_all = par_rows * lax.axis_size(SPACE)
    moved, parts = lax.optimization_barrier((shifted(sent, 1), parts))
    coarse = in_vmem(coarse_kernel, bf16((par_rows, out_chans)), (own, moved, down_weight), "coarse")
    down_grad = finished(parts, 1.0 / math.sqrt(worlds_all * parents_all))
    return (fine[None], coarse[None], down_grad)


def solution(mesh):
    return jax.shard_map(
        body,
        mesh=split_mesh(mesh),
        in_specs=(
            P(DP, SPACE, None),
            P(DP, None, SPACE),
            P(DP, SPACE),
            P(),
            P(),
            P(),
            P(),
            P(),
            P(DP, SPACE, None),
        ),
        out_specs=(P(DP, SPACE, None), P(DP, SPACE, None), P()),
        check_vma=False,
    )
```

```python
import functools
import math

import jax
import jax.numpy as jnp
from jax import lax
from jax.experimental import pallas as pl
from jax.experimental.pallas import tpu as pltpu
from jax.sharding import Mesh
from jax.sharding import PartitionSpec as P


DP = "y"
SPACE = ("z", "x", "core")
PLANE = ("y", "x", "core")
GROUP = 3
VMEM_BYTES = 32 << 20
PAR_ROWS = 64
COST_BYTES = 1 << 20


def split_mesh(mesh):
    dp, space = mesh.devices.shape
    return Mesh(mesh.devices.reshape(dp, space // 8, 4, 2), (DP,) + SPACE)


def shifted(array, by):
    length = lax.axis_size(SPACE)
    return lax.ppermute(array, SPACE, [(i, (i + by) % length) for i in range(length)])


def from_partner(array):
    length = lax.axis_size(SPACE)
    return lax.ppermute(array, SPACE, [(i, i ^ 1) for i in range(length)])


def settled(running, gain):
    inverse = lax.rsqrt(jnp.mean(running * running, axis=-1, keepdims=True) + 1e-05)
    scaled = running * inverse * gain
    return scaled / (1.0 + jnp.exp(-scaled))


def local_table(taps_ref):
    taps, _, rows = taps_ref.shape
    lowest = (lax.axis_index(SPACE) - 1) * rows
    ids = taps_ref[...].reshape(taps, rows)
    local = jnp.where(ids < 0, -4 * rows, ids - lowest)
    return jnp.concatenate([local, jnp.full((-taps % 8, rows), -1, jnp.int32)], axis=0).T


def pick(local, taps, blocks, select_ref, put, wait=None):
    rows = local.shape[0]
    places = lax.broadcasted_iota(jnp.int16, (rows, rows), 1)
    one, zero = jnp.ones((), jnp.bfloat16), jnp.zeros((), jnp.bfloat16)
    for tap in range(taps):
        column = jnp.broadcast_to(local[:, tap : tap + 1], (rows, 128))
        for b, (_, start) in enumerate(blocks):
            wanted = (column - start).astype(jnp.int16)
            wanted = jnp.concatenate([wanted] * (rows // 128), axis=1)
            select_ref[tap * rows : (tap + 1) * rows, b * rows : (b + 1) * rows] = jnp.where(
                wanted == places, one, zero
            )
    if wait is not None:
        wait()
    for first in range(0, taps, GROUP):
        part = select_ref[first * rows : (first + GROUP) * rows]
        picked = sum(
            jnp.dot(part[:, b * rows : (b + 1) * rows], block[...], preferred_element_type=jnp.float32)
            for b, (block, _) in enumerate(blocks)
        ).astype(jnp.bfloat16)
        for j in range(GROUP):
            put(first + j, picked[j * rows : (j + 1) * rows])


def pick_near(local, here, partner, select_ref, near_ref, wait=None):
    rows, chans = here.shape
    blocks = ((here, rows), (partner, 2 * rows * (1 - lax.axis_index("core"))))

    def put(tap, picked):
        near_ref[:, tap * chans : (tap + 1) * chans] = picked

    pick(local, near_ref.shape[1] // chans, blocks, select_ref, put, wait)


def convolved(local, before, after, near_ref, weight_ref, select_ref, picked_ref):
    rows, chans = before.shape
    across = jnp.where(lax.axis_index("core") == 1, after, before)
    taps = weight_ref.shape[0]

    def put(tap, picked):
        columns = slice(tap * chans, (tap + 1) * chans)
        picked_ref[:, columns] = near_ref[:, columns] + picked

    pick(local, taps, ((across, 2 * rows * lax.axis_index("core")),), select_ref, put)
    return jnp.dot(
        picked_ref[...],
        weight_ref[...].reshape(taps * chans, weight_ref.shape[2]),
        preferred_element_type=jnp.float32,
    )


def first_near_kernel(
    partner, taps_hbm, here_hbm, near_ref, local_ref, select_ref, taps_ref, here, taps_sem, here_sem
):
    taps_copy = pltpu.make_async_copy(taps_hbm, taps_ref, taps_sem)
    here_copy = pltpu.make_async_copy(here_hbm, here, here_sem)
    taps_copy.start()
    here_copy.start()
    taps_copy.wait()
    local = local_table(taps_ref)
    local_ref[...] = local
    pick_near(local, here, partner, select_ref, near_ref, here_copy.wait)


def first_far_kernel(
    local_ref, after, before, near_ref, weight_ref, gain_ref, parent_ref,
    middle_ref, select_ref, picked_ref,
):
    total = convolved(local_ref[...], before[...], after[...], near_ref, weight_ref, select_ref, picked_ref)
    rows = total.shape[0]
    middle_ref[:rows] = settled(total, gain_ref[...]).astype(middle_ref.dtype)
    ids = parent_ref[...] - lax.axis_index(SPACE) * PAR_ROWS
    ids = jnp.broadcast_to(ids.astype(jnp.float32), (middle_ref.shape[0] - rows, ids.shape[1]))
    middle_ref[rows:] = ids.astype(middle_ref.dtype)


def second_near_kernel(local_ref, here, partner, near_ref, select_ref):
    rows = local_ref.shape[0]
    pick_near(local_ref[...], here[:rows], partner[:rows], select_ref, near_ref)


def membership(ids, parents):
    return (lax.broadcasted_iota(jnp.int32, (parents, ids.shape[1]), 0) == ids).astype(jnp.float32)


def second_far_kernel(
    local_ref, after, before, near_ref, weight_ref, gain_ref, feature_ref, parent_ref,
    cotangent_ref, next_ref,
    fine_ref, own_ref, sent_ref, grad_ref, select_ref, picked_ref,
):
    rows, chans = feature_ref.shape
    total = convolved(local_ref[...], before[:rows], after[:rows], near_ref, weight_ref, select_ref, picked_ref)
    fine = feature_ref[...].astype(jnp.float32) + settled(total, gain_ref[...])
    fine = fine.astype(fine_ref.dtype)
    fine_ref[...] = fine
    half = cotangent_ref.shape[0]
    member = membership(parent_ref[...] - lax.axis_index(SPACE) * half, 2 * half)
    sums = jnp.dot(member.astype(jnp.bfloat16), fine, preferred_element_type=jnp.float32)

    def tally(ids):
        return jnp.sum(membership(ids, 2 * half), axis=1, keepdims=True)

    tally_own = jnp.sum(member, axis=1, keepdims=True)
    tally_before = tally(before[rows:].astype(jnp.float32)[:1].astype(jnp.int32))[half:]
    tally_after = tally(after[rows:].astype(jnp.float32)[:1].astype(jnp.int32))[:half]
    count_own = jnp.maximum(tally_own[:half] + tally_before, 1.0)
    count_after = jnp.maximum(tally_own[half:] + tally_after, 1.0)
    own_ref[:, :chans] = sums[:half]
    own_ref[:, chans:] = jnp.broadcast_to(count_own, (half, own_ref.shape[1] - chans))
    sent_ref[...] = sums[half:]
    shares = sums / jnp.concatenate([count_own, count_after], axis=0)
    grads_in = jnp.concatenate([cotangent_ref[...], next_ref[...]], axis=0)
    grad_ref[...] = lax.dot_general(
        shares.astype(jnp.bfloat16), grads_in, (((0,), (0,)), ((), ())), preferred_element_type=jnp.float32
    ).astype(grad_ref.dtype)


def last_kernel(own_ref, moved_ref, down_ref, gathered_ref, coarse_ref, grad_ref):
    grad_ref[...] = gathered_ref[...].astype(grad_ref.dtype)
    chans = down_ref.shape[0]
    own = own_ref[...]
    pooled = ((own[:, :chans] + moved_ref[...]) / own[:, chans : chans + 1]).astype(jnp.bfloat16)
    coarse_ref[...] = jnp.dot(pooled, down_ref[...], preferred_element_type=jnp.float32).astype(coarse_ref.dtype)


def in_vmem(kernel, outs, inputs, name, scratch=(), flops=0, from_hbm=()):
    vmem = pl.BlockSpec(memory_space=pltpu.VMEM)
    return pl.pallas_call(
        kernel,
        out_shape=outs,
        in_specs=[vmem] * len(inputs) + [pl.BlockSpec(memory_space=pltpu.HBM)] * len(from_hbm),
        out_specs=jax.tree.map(lambda _: vmem, outs),
        scratch_shapes=scratch,
        compiler_params=pltpu.CompilerParams(vmem_limit_bytes=VMEM_BYTES),
        cost_estimate=pl.CostEstimate(flops=flops, bytes_accessed=COST_BYTES, transcendentals=0),
        name=name,
    )(*inputs, *[pltpu.with_memory_space_constraint(array, pltpu.HBM) for array in from_hbm])


def exchanged(pieces, axes):
    return lax.all_to_all(pieces, axes, 0, 0, tiled=True)


def plane_summed(local_grad):
    rows, cols = local_grad.shape
    plane = lax.axis_size(PLANE)
    return exchanged(local_grad.reshape(plane, rows // plane, cols), PLANE)


def space_summed(parts, scale):
    part = jnp.sum(parts.astype(jnp.float32), axis=0)
    copies = jnp.broadcast_to(part[None], (lax.axis_size("z"),) + part.shape)
    return jnp.sum(exchanged(copies, "z"), axis=0) * scale


def gathered(part):
    copies = jnp.broadcast_to(part.astype(jnp.bfloat16)[None], (lax.axis_size(PLANE),) + part.shape)
    return exchanged(copies, PLANE).reshape(-1, part.shape[1])


def body(
    features,
    neighbours,
    parents,
    conv_first,
    conv_second,
    gain_first,
    gain_second,
    down_weight,
    cotangent,
):
    field, grad_in = features[0], cotangent[0]
    _, taps, rows = neighbours.shape
    chans = field.shape[1]
    par_rows, out_chans = grad_in.shape
    bf16 = functools.partial(jax.ShapeDtypeStruct, dtype=jnp.bfloat16)
    f32 = functools.partial(jax.ShapeDtypeStruct, dtype=jnp.float32)
    product = 2 * taps * rows * chans * rows
    near_shape = bf16((rows, taps * chans))
    select = [pltpu.VMEM((taps * rows, 2 * rows), jnp.bfloat16)]
    select_and_picked = [
        pltpu.VMEM((taps * rows, rows), jnp.bfloat16),
        pltpu.VMEM((rows, taps * chans), jnp.bfloat16),
    ]
    after, before = shifted(field, -1), shifted(field, 1)
    near, local = in_vmem(
        first_near_kernel,
        (near_shape, jax.ShapeDtypeStruct((rows, taps + -taps % 8), jnp.int32)),
        (from_partner(field),),
        "first_near",
        select
        + [
            pltpu.VMEM((taps, 1, rows), jnp.int32),
            pltpu.VMEM((rows, chans), jnp.bfloat16),
            pltpu.SemaphoreType.DMA,
            pltpu.SemaphoreType.DMA,
        ],
        2 * product,
        (jnp.moveaxis(neighbours, 1, 0), field),
    )
    ready, near = lax.optimization_barrier((grad_in, near))
    next_grad = shifted(ready, -1)
    middle = in_vmem(
        first_far_kernel,
        bf16((rows + 16, chans)),
        (local, after, before, near, conv_first, gain_first[None], parents),
        "first_far", select_and_picked, 2 * product,
    )
    middle, next_grad = lax.optimization_barrier((middle, next_grad))
    after, before = shifted(middle, -1), shifted(middle, 1)
    partner = from_partner(middle)
    near = in_vmem(
        second_near_kernel, near_shape, (local, middle, partner), "second_near", select, 2 * product
    )
    fine, own, sent, local_grad = in_vmem(
        second_far_kernel,
        (
            bf16((rows, chans)),
            f32((par_rows, chans + 128)),
            f32((par_rows, chans)),
            bf16((chans, out_chans)),
        ),
        (
            local, after, before, near, conv_second, gain_second[None], field, parents,
            grad_in, next_grad,
        ),
        "second_far", select_and_picked, 2 * product,
    )
    worlds_all = lax.axis_size(DP)
    parents_all = par_rows * lax.axis_size(SPACE)
    part = space_summed(plane_summed(local_grad), 1.0 / math.sqrt(worlds_all * parents_all))
    sent, part = lax.optimization_barrier((sent, part))
    coarse, down_grad = in_vmem(
        last_kernel,
        (bf16((par_rows, out_chans)), f32((chans, out_chans))),
        (own, shifted(sent, 1), down_weight, gathered(part)),
        "coarse_and_grad",
    )
    return (fine[None], coarse[None], down_grad)


def solution(mesh):
    return jax.shard_map(
        body,
        mesh=split_mesh(mesh),
        in_specs=(
            P(DP, SPACE, None),
            P(DP, None, SPACE),
            P(DP, SPACE),
            P(),
            P(),
            P(),
            P(),
            P(),
            P(DP, SPACE, None),
        ),
        out_specs=(P(DP, SPACE, None), P(DP, SPACE, None), P()),
        check_vma=False,
    )
```

```python
import functools
import math

import jax
import jax.numpy as jnp
from jax import lax
from jax.experimental import pallas as pl
from jax.experimental.pallas import tpu as pltpu
from jax.sharding import Mesh
from jax.sharding import PartitionSpec as P


DP = "y"
SPACE = ("z", "x", "core")
PLANE = ("y", "x", "core")
CHIPS = ("y", "x")
GROUP = 3
VMEM_BYTES = 32 << 20
PAR_ROWS = 64
COST_BYTES = 1 << 20


def split_mesh(mesh):
    dp, space = mesh.devices.shape
    return Mesh(mesh.devices.reshape(dp, space // 8, 4, 2), (DP,) + SPACE)


def shifted(array, by):
    length = lax.axis_size(SPACE)
    return lax.ppermute(array, SPACE, [(i, (i + by) % length) for i in range(length)])


def from_partner(array):
    length = lax.axis_size(SPACE)
    return lax.ppermute(array, SPACE, [(i, i ^ 1) for i in range(length)])


def settled(running, gain):
    inverse = lax.rsqrt(jnp.mean(running * running, axis=-1, keepdims=True) + 1e-05)
    scaled = running * inverse * gain
    return scaled / (1.0 + jnp.exp(-scaled))


def local_table(taps_ref):
    taps, _, rows = taps_ref.shape
    lowest = (lax.axis_index(SPACE) - 1) * rows
    ids = taps_ref[...].reshape(taps, rows)
    local = jnp.where(ids < 0, -4 * rows, ids - lowest)
    return jnp.concatenate([local, jnp.full((-taps % 8, rows), -1, jnp.int32)], axis=0).T


def pick(local, taps, blocks, select_ref, put, wait=None):
    rows = local.shape[0]
    places = lax.broadcasted_iota(jnp.int16, (rows, rows), 1)
    one, zero = jnp.ones((), jnp.bfloat16), jnp.zeros((), jnp.bfloat16)
    for tap in range(taps):
        column = jnp.broadcast_to(local[:, tap : tap + 1], (rows, 128))
        for b, (_, start) in enumerate(blocks):
            wanted = (column - start).astype(jnp.int16)
            wanted = jnp.concatenate([wanted] * (rows // 128), axis=1)
            select_ref[tap * rows : (tap + 1) * rows, b * rows : (b + 1) * rows] = jnp.where(
                wanted == places, one, zero
            )
    if wait is not None:
        wait()
    for first in range(0, taps, GROUP):
        part = select_ref[first * rows : (first + GROUP) * rows]
        picked = sum(
            jnp.dot(part[:, b * rows : (b + 1) * rows], block[...], preferred_element_type=jnp.float32)
            for b, (block, _) in enumerate(blocks)
        ).astype(jnp.bfloat16)
        for j in range(GROUP):
            put(first + j, picked[j * rows : (j + 1) * rows])


def pick_near(local, here, partner, select_ref, near_ref, wait=None):
    rows, chans = here.shape
    blocks = ((here, rows), (partner, 2 * rows * (1 - lax.axis_index("core"))))

    def put(tap, picked):
        near_ref[:, tap * chans : (tap + 1) * chans] = picked

    pick(local, near_ref.shape[1] // chans, blocks, select_ref, put, wait)


def convolved(local, before, after, near_ref, weight_ref, select_ref, picked_ref):
    rows, chans = before.shape
    across = jnp.where(lax.axis_index("core") == 1, after, before)
    taps = weight_ref.shape[0]

    def put(tap, picked):
        columns = slice(tap * chans, (tap + 1) * chans)
        picked_ref[:, columns] = near_ref[:, columns] + picked

    pick(local, taps, ((across, 2 * rows * lax.axis_index("core")),), select_ref, put)
    return jnp.dot(
        picked_ref[...],
        weight_ref[...].reshape(taps * chans, weight_ref.shape[2]),
        preferred_element_type=jnp.float32,
    )


def first_near_kernel(
    partner, taps_hbm, here_hbm, near_ref, local_ref, select_ref, taps_ref, here, taps_sem, here_sem
):
    taps_copy = pltpu.make_async_copy(taps_hbm, taps_ref, taps_sem)
    here_copy = pltpu.make_async_copy(here_hbm, here, here_sem)
    taps_copy.start()
    here_copy.start()
    taps_copy.wait()
    local = local_table(taps_ref)
    local_ref[...] = local
    pick_near(local, here, partner, select_ref, near_ref, here_copy.wait)


def first_far_kernel(
    local_ref, after, before, near_ref, weight_ref, gain_ref, parent_ref,
    middle_ref, select_ref, picked_ref,
):
    total = convolved(local_ref[...], before[...], after[...], near_ref, weight_ref, select_ref, picked_ref)
    rows = total.shape[0]
    middle_ref[:rows] = settled(total, gain_ref[...]).astype(middle_ref.dtype)
    ids = parent_ref[...] - lax.axis_index(SPACE) * PAR_ROWS
    ids = jnp.broadcast_to(ids.astype(jnp.float32), (middle_ref.shape[0] - rows, ids.shape[1]))
    middle_ref[rows:] = ids.astype(middle_ref.dtype)


def second_near_kernel(local_ref, here, partner, near_ref, select_ref):
    rows = local_ref.shape[0]
    pick_near(local_ref[...], here[:rows], partner[:rows], select_ref, near_ref)


def membership(ids, parents):
    return (lax.broadcasted_iota(jnp.int32, (parents, ids.shape[1]), 0) == ids).astype(jnp.float32)


def second_far_kernel(
    local_ref, after, before, near_ref, weight_ref, gain_ref, feature_ref, parent_ref,
    cotangent_ref, next_ref,
    fine_ref, own_ref, sent_ref, grad_ref, select_ref, picked_ref,
):
    rows, chans = feature_ref.shape
    total = convolved(local_ref[...], before[:rows], after[:rows], near_ref, weight_ref, select_ref, picked_ref)
    fine = feature_ref[...].astype(jnp.float32) + settled(total, gain_ref[...])
    fine = fine.astype(fine_ref.dtype)
    fine_ref[...] = fine
    half = cotangent_ref.shape[0]
    member = membership(parent_ref[...] - lax.axis_index(SPACE) * half, 2 * half)
    sums = jnp.dot(member.astype(jnp.bfloat16), fine, preferred_element_type=jnp.float32)

    def tally(ids):
        return jnp.sum(membership(ids, 2 * half), axis=1, keepdims=True)

    tally_own = jnp.sum(member, axis=1, keepdims=True)
    tally_before = tally(before[rows:].astype(jnp.float32)[:1].astype(jnp.int32))[half:]
    tally_after = tally(after[rows:].astype(jnp.float32)[:1].astype(jnp.int32))[:half]
    count_own = jnp.maximum(tally_own[:half] + tally_before, 1.0)
    count_after = jnp.maximum(tally_own[half:] + tally_after, 1.0)
    own_ref[:, :chans] = sums[:half]
    own_ref[:, chans:] = jnp.broadcast_to(count_own, (half, own_ref.shape[1] - chans))
    sent_ref[...] = sums[half:]
    shares = sums / jnp.concatenate([count_own, count_after], axis=0)
    grads_in = jnp.concatenate([cotangent_ref[...], next_ref[...]], axis=0)
    grad_ref[...] = lax.dot_general(
        shares.astype(jnp.bfloat16), grads_in, (((0,), (0,)), ((), ())), preferred_element_type=jnp.float32
    ).astype(grad_ref.dtype)


def spread_kernel(scale, parts_ref, copies_ref):
    total = jnp.sum(parts_ref[...], axis=0) * scale
    copies_ref[...] = jnp.broadcast_to(total.astype(copies_ref.dtype)[None], copies_ref.shape)


def last_kernel(own_ref, moved_ref, down_ref, mine_ref, other_ref, coarse_ref, grad_ref):
    mine, other = mine_ref[...], other_ref[...]
    upper = lax.axis_index("core") == 1
    grad_ref[:, 0] = jnp.where(upper, other, mine).astype(grad_ref.dtype)
    grad_ref[:, 1] = jnp.where(upper, mine, other).astype(grad_ref.dtype)
    chans = down_ref.shape[0]
    own = own_ref[...]
    pooled = ((own[:, :chans] + moved_ref[...]) / own[:, chans : chans + 1]).astype(jnp.bfloat16)
    coarse_ref[...] = jnp.dot(pooled, down_ref[...], preferred_element_type=jnp.float32).astype(coarse_ref.dtype)


def in_vmem(kernel, outs, inputs, name, scratch=(), flops=0, from_hbm=()):
    vmem = pl.BlockSpec(memory_space=pltpu.VMEM)
    return pl.pallas_call(
        kernel,
        out_shape=outs,
        in_specs=[vmem] * len(inputs) + [pl.BlockSpec(memory_space=pltpu.HBM)] * len(from_hbm),
        out_specs=jax.tree.map(lambda _: vmem, outs),
        scratch_shapes=scratch,
        compiler_params=pltpu.CompilerParams(vmem_limit_bytes=VMEM_BYTES),
        cost_estimate=pl.CostEstimate(flops=flops, bytes_accessed=COST_BYTES, transcendentals=0),
        name=name,
    )(*inputs, *[pltpu.with_memory_space_constraint(array, pltpu.HBM) for array in from_hbm])


def exchanged(pieces, axes):
    return lax.all_to_all(pieces, axes, 0, 0, tiled=True)


def plane_summed(local_grad):
    rows, cols = local_grad.shape
    plane = lax.axis_size(PLANE)
    return exchanged(local_grad.reshape(plane, rows // plane, cols), PLANE)


def space_parts(parts):
    part = jnp.sum(parts.astype(jnp.float32), axis=0)
    return exchanged(jnp.broadcast_to(part[None], (lax.axis_size("z"),) + part.shape), "z")


def body(
    features,
    neighbours,
    parents,
    conv_first,
    conv_second,
    gain_first,
    gain_second,
    down_weight,
    cotangent,
):
    field, grad_in = features[0], cotangent[0]
    _, taps, rows = neighbours.shape
    chans = field.shape[1]
    par_rows, out_chans = grad_in.shape
    bf16 = functools.partial(jax.ShapeDtypeStruct, dtype=jnp.bfloat16)
    f32 = functools.partial(jax.ShapeDtypeStruct, dtype=jnp.float32)
    product = 2 * taps * rows * chans * rows
    near_shape = bf16((rows, taps * chans))
    select = [pltpu.VMEM((taps * rows, 2 * rows), jnp.bfloat16)]
    select_and_picked = [
        pltpu.VMEM((taps * rows, rows), jnp.bfloat16),
        pltpu.VMEM((rows, taps * chans), jnp.bfloat16),
    ]
    after, before = shifted(field, -1), shifted(field, 1)
    near, local = in_vmem(
        first_near_kernel,
        (near_shape, jax.ShapeDtypeStruct((rows, taps + -taps % 8), jnp.int32)),
        (from_partner(field),),
        "first_near",
        select
        + [
            pltpu.VMEM((taps, 1, rows), jnp.int32),
            pltpu.VMEM((rows, chans), jnp.bfloat16),
            pltpu.SemaphoreType.DMA,
            pltpu.SemaphoreType.DMA,
        ],
        2 * product,
        (jnp.moveaxis(neighbours, 1, 0), field),
    )
    ready, near = lax.optimization_barrier((grad_in, near))
    next_grad = shifted(ready, -1)
    middle = in_vmem(
        first_far_kernel,
        bf16((rows + 16, chans)),
        (local, after, before, near, conv_first, gain_first[None], parents),
        "first_far", select_and_picked, 2 * product,
    )
    middle, next_grad = lax.optimization_barrier((middle, next_grad))
    after, before = shifted(middle, -1), shifted(middle, 1)
    partner = from_partner(middle)
    near = in_vmem(
        second_near_kernel, near_shape, (local, middle, partner), "second_near", select, 2 * product
    )
    fine, own, sent, local_grad = in_vmem(
        second_far_kernel,
        (
            bf16((rows, chans)),
            f32((par_rows, chans + 128)),
            f32((par_rows, chans)),
            bf16((chans, out_chans)),
        ),
        (
            local, after, before, near, conv_second, gain_second[None], field, parents,
            grad_in, next_grad,
        ),
        "second_far", select_and_picked, 2 * product,
    )
    worlds_all = lax.axis_size(DP)
    parents_all = par_rows * lax.axis_size(SPACE)
    parts = space_parts(plane_summed(local_grad))
    sent, parts = lax.optimization_barrier((sent, parts))
    chips = lax.axis_size(CHIPS)
    copies = in_vmem(
        functools.partial(spread_kernel, 1.0 / math.sqrt(worlds_all * parents_all)),
        bf16((chips,) + parts.shape[1:]),
        (parts,),
        "spread",
    )
    mine, moved = lax.optimization_barrier((exchanged(copies, CHIPS), shifted(sent, 1)))
    coarse, down_grad = in_vmem(
        last_kernel,
        (bf16((par_rows, out_chans)), f32((chips, lax.axis_size("core")) + mine.shape[1:])),
        (own, moved, down_weight, mine, from_partner(mine)),
        "coarse_and_grad",
    )
    down_grad = down_grad.reshape(chans, out_chans)
    return (fine[None], coarse[None], down_grad)


def solution(mesh):
    return jax.shard_map(
        body,
        mesh=split_mesh(mesh),
        in_specs=(
            P(DP, SPACE, None),
            P(DP, None, SPACE),
            P(DP, SPACE),
            P(),
            P(),
            P(),
            P(),
            P(),
            P(DP, SPACE, None),
        ),
        out_specs=(P(DP, SPACE, None), P(DP, SPACE, None), P()),
        check_vma=False,
    )
```

```python
import functools
import math

import jax
import jax.numpy as jnp
from jax import lax
from jax.experimental import pallas as pl
from jax.experimental.pallas import tpu as pltpu
from jax.sharding import Mesh
from jax.sharding import PartitionSpec as P


DP = "y"
SPACE = ("z", "x", "core")
PLANE = ("y", "x", "core")
GROUP = 3
VMEM_BYTES = 32 << 20
PAR_ROWS = 64
COST_BYTES = 1 << 20


def split_mesh(mesh):
    dp, space = mesh.devices.shape
    return Mesh(mesh.devices.reshape(dp, space // 8, 4, 2), (DP,) + SPACE)


def shifted(array, by):
    length = lax.axis_size(SPACE)
    return lax.ppermute(array, SPACE, [(i, (i + by) % length) for i in range(length)])


def from_partner(array):
    length = lax.axis_size(SPACE)
    return lax.ppermute(array, SPACE, [(i, i ^ 1) for i in range(length)])


def settled(running, gain):
    inverse = lax.rsqrt(jnp.mean(running * running, axis=-1, keepdims=True) + 1e-05)
    scaled = running * inverse * gain
    return scaled / (1.0 + jnp.exp(-scaled))


def local_table(taps_ref):
    taps, _, rows = taps_ref.shape
    lowest = (lax.axis_index(SPACE) - 1) * rows
    ids = taps_ref[...].reshape(taps, rows)
    local = jnp.where(ids < 0, -4 * rows, ids - lowest)
    return jnp.concatenate([local, jnp.full((-taps % 8, rows), -1, jnp.int32)], axis=0).T


def select(local, taps, starts, select_ref):
    rows = local.shape[0]
    places = lax.broadcasted_iota(jnp.int16, (rows, rows), 1)
    one, zero = jnp.ones((), jnp.bfloat16), jnp.zeros((), jnp.bfloat16)
    for tap in range(taps):
        column = jnp.broadcast_to(local[:, tap : tap + 1], (rows, 128))
        for b, start in enumerate(starts):
            wanted = (column - start).astype(jnp.int16)
            wanted = jnp.concatenate([wanted] * (rows // 128), axis=1)
            select_ref[tap * rows : (tap + 1) * rows, b * rows : (b + 1) * rows] = jnp.where(
                wanted == places, one, zero
            )


def pick(taps, blocks, select_ref, put):
    rows = blocks[0].shape[0]
    for first in range(0, taps, GROUP):
        part = select_ref[first * rows : (first + GROUP) * rows]
        picked = sum(
            jnp.dot(part[:, b * rows : (b + 1) * rows], block[...], preferred_element_type=jnp.float32)
            for b, block in enumerate(blocks)
        ).astype(jnp.bfloat16)
        for j in range(GROUP):
            put(first + j, picked[j * rows : (j + 1) * rows])


def pick_near(local, here, partner, select_ref, near_ref, wait=None):
    rows, chans = here.shape
    taps = near_ref.shape[1] // chans
    select(local, taps, (rows, 2 * rows * (1 - lax.axis_index("core"))), select_ref)

    def put(tap, picked):
        near_ref[:, tap * chans : (tap + 1) * chans] = picked

    if wait is not None:
        wait()
    pick(taps, (here, partner), select_ref, put)


def convolved(select_ref, before, after, near_ref, weight_ref, picked_ref):
    chans = before.shape[1]
    across = jnp.where(lax.axis_index("core") == 1, after, before)
    taps = weight_ref.shape[0]

    def put(tap, picked):
        columns = slice(tap * chans, (tap + 1) * chans)
        picked_ref[:, columns] = near_ref[:, columns] + picked

    pick(taps, (across,), select_ref, put)
    return jnp.dot(
        picked_ref[...],
        weight_ref[...].reshape(taps * chans, weight_ref.shape[2]),
        preferred_element_type=jnp.float32,
    )


def first_near_kernel(
    partner, taps_hbm, here_hbm, near_ref, local_ref, far_ref, select_ref, taps_ref, here, taps_sem, here_sem
):
    taps_copy = pltpu.make_async_copy(taps_hbm, taps_ref, taps_sem)
    here_copy = pltpu.make_async_copy(here_hbm, here, here_sem)
    taps_copy.start()
    here_copy.start()
    taps_copy.wait()
    local = local_table(taps_ref)
    local_ref[...] = local
    pick_near(local, here, partner, select_ref, near_ref, here_copy.wait)
    rows = here.shape[0]
    select(local, taps_ref.shape[0], (2 * rows * lax.axis_index("core"),), far_ref)


def first_far_kernel(
    select_ref, after, before, near_ref, weight_ref, gain_ref, parent_ref, middle_ref, picked_ref
):
    total = convolved(select_ref, before[...], after[...], near_ref, weight_ref, picked_ref)
    rows = total.shape[0]
    middle_ref[:rows] = settled(total, gain_ref[...]).astype(middle_ref.dtype)
    ids = parent_ref[...] - lax.axis_index(SPACE) * PAR_ROWS
    ids = jnp.broadcast_to(ids.astype(jnp.float32), (middle_ref.shape[0] - rows, ids.shape[1]))
    middle_ref[rows:] = ids.astype(middle_ref.dtype)


def second_near_kernel(local_ref, here, partner, near_ref, select_ref):
    rows = local_ref.shape[0]
    pick_near(local_ref[...], here[:rows], partner[:rows], select_ref, near_ref)


def membership(ids, parents):
    return (lax.broadcasted_iota(jnp.int32, (parents, ids.shape[1]), 0) == ids).astype(jnp.float32)


def second_far_kernel(
    select_ref, after, before, near_ref, weight_ref, gain_ref, feature_ref, parent_ref,
    cotangent_ref, next_ref,
    fine_ref, own_ref, sent_ref, grad_ref, picked_ref,
):
    rows, chans = feature_ref.shape
    total = convolved(select_ref, before[:rows], after[:rows], near_ref, weight_ref, picked_ref)
    fine = feature_ref[...].astype(jnp.float32) + settled(total, gain_ref[...])
    fine = fine.astype(fine_ref.dtype)
    fine_ref[...] = fine
    half = cotangent_ref.shape[0]
    member = membership(parent_ref[...] - lax.axis_index(SPACE) * half, 2 * half)
    sums = jnp.dot(member.astype(jnp.bfloat16), fine, preferred_element_type=jnp.float32)

    def tally(ids):
        return jnp.sum(membership(ids, 2 * half), axis=1, keepdims=True)

    tally_own = jnp.sum(member, axis=1, keepdims=True)
    tally_before = tally(before[rows:].astype(jnp.float32)[:1].astype(jnp.int32))[half:]
    tally_after = tally(after[rows:].astype(jnp.float32)[:1].astype(jnp.int32))[:half]
    count_own = jnp.maximum(tally_own[:half] + tally_before, 1.0)
    count_after = jnp.maximum(tally_own[half:] + tally_after, 1.0)
    own_ref[:, :chans] = sums[:half]
    own_ref[:, chans:] = jnp.broadcast_to(count_own, (half, own_ref.shape[1] - chans))
    sent_ref[...] = sums[half:]
    shares = sums / jnp.concatenate([count_own, count_after], axis=0)
    grads_in = jnp.concatenate([cotangent_ref[...], next_ref[...]], axis=0)
    grad_ref[...] = lax.dot_general(
        shares.astype(jnp.bfloat16), grads_in, (((0,), (0,)), ((), ())), preferred_element_type=jnp.float32
    ).astype(grad_ref.dtype)


def last_kernel(own_ref, moved_ref, down_ref, gathered_ref, coarse_ref, grad_ref):
    grad_ref[...] = gathered_ref[...].astype(grad_ref.dtype)
    chans = down_ref.shape[0]
    own = own_ref[...]
    pooled = ((own[:, :chans] + moved_ref[...]) / own[:, chans : chans + 1]).astype(jnp.bfloat16)
    coarse_ref[...] = jnp.dot(pooled, down_ref[...], preferred_element_type=jnp.float32).astype(coarse_ref.dtype)


def in_vmem(kernel, outs, inputs, name, scratch=(), flops=0, from_hbm=()):
    vmem = pl.BlockSpec(memory_space=pltpu.VMEM)
    return pl.pallas_call(
        kernel,
        out_shape=outs,
        in_specs=[vmem] * len(inputs) + [pl.BlockSpec(memory_space=pltpu.HBM)] * len(from_hbm),
        out_specs=jax.tree.map(lambda _: vmem, outs),
        scratch_shapes=scratch,
        compiler_params=pltpu.CompilerParams(vmem_limit_bytes=VMEM_BYTES),
        cost_estimate=pl.CostEstimate(flops=flops, bytes_accessed=COST_BYTES, transcendentals=0),
        name=name,
    )(*inputs, *[pltpu.with_memory_space_constraint(array, pltpu.HBM) for array in from_hbm])


def exchanged(pieces, axes):
    return lax.all_to_all(pieces, axes, 0, 0, tiled=True)


def plane_summed(local_grad):
    rows, cols = local_grad.shape
    plane = lax.axis_size(PLANE)
    return exchanged(local_grad.reshape(plane, rows // plane, cols), PLANE)


def space_summed(parts, scale):
    part = jnp.sum(parts.astype(jnp.float32), axis=0)
    copies = jnp.broadcast_to(part[None], (lax.axis_size("z"),) + part.shape)
    return jnp.sum(exchanged(copies, "z"), axis=0) * scale


def gathered(part):
    copies = jnp.broadcast_to(part.astype(jnp.bfloat16)[None], (lax.axis_size(PLANE),) + part.shape)
    return exchanged(copies, PLANE).reshape(-1, part.shape[1])


def body(
    features,
    neighbours,
    parents,
    conv_first,
    conv_second,
    gain_first,
    gain_second,
    down_weight,
    cotangent,
):
    field, grad_in = features[0], cotangent[0]
    _, taps, rows = neighbours.shape
    chans = field.shape[1]
    par_rows, out_chans = grad_in.shape
    bf16 = functools.partial(jax.ShapeDtypeStruct, dtype=jnp.bfloat16)
    f32 = functools.partial(jax.ShapeDtypeStruct, dtype=jnp.float32)
    product = 2 * taps * rows * chans * rows
    near_shape = bf16((rows, taps * chans))
    chosen = [pltpu.VMEM((taps * rows, 2 * rows), jnp.bfloat16)]
    all_picked = [pltpu.VMEM((rows, taps * chans), jnp.bfloat16)]
    after, before = shifted(field, -1), shifted(field, 1)
    near, local, far = in_vmem(
        first_near_kernel,
        (
            near_shape,
            jax.ShapeDtypeStruct((rows, taps + -taps % 8), jnp.int32),
            bf16((taps * rows, rows)),
        ),
        (from_partner(field),),
        "first_near",
        chosen
        + [
            pltpu.VMEM((taps, 1, rows), jnp.int32),
            pltpu.VMEM((rows, chans), jnp.bfloat16),
            pltpu.SemaphoreType.DMA,
            pltpu.SemaphoreType.DMA,
        ],
        2 * product,
        (jnp.moveaxis(neighbours, 1, 0), field),
    )
    ready, near = lax.optimization_barrier((grad_in, near))
    next_grad = shifted(ready, -1)
    middle = in_vmem(
        first_far_kernel,
        bf16((rows + 16, chans)),
        (far, after, before, near, conv_first, gain_first[None], parents),
        "first_far", all_picked, 2 * product,
    )
    middle, next_grad = lax.optimization_barrier((middle, next_grad))
    after, before = shifted(middle, -1), shifted(middle, 1)
    partner = from_partner(middle)
    near = in_vmem(
        second_near_kernel, near_shape, (local, middle, partner), "second_near", chosen, 2 * product
    )
    fine, own, sent, local_grad = in_vmem(
        second_far_kernel,
        (
            bf16((rows, chans)),
            f32((par_rows, chans + 128)),
            f32((par_rows, chans)),
            bf16((chans, out_chans)),
        ),
        (
            far, after, before, near, conv_second, gain_second[None], field, parents,
            grad_in, next_grad,
        ),
        "second_far", all_picked, 2 * product,
    )
    worlds_all = lax.axis_size(DP)
    parents_all = par_rows * lax.axis_size(SPACE)
    part = space_summed(plane_summed(local_grad), 1.0 / math.sqrt(worlds_all * parents_all))
    sent, part = lax.optimization_barrier((sent, part))
    coarse, down_grad = in_vmem(
        last_kernel,
        (bf16((par_rows, out_chans)), f32((chans, out_chans))),
        (own, shifted(sent, 1), down_weight, gathered(part)),
        "coarse_and_grad",
    )
    return (fine[None], coarse[None], down_grad)


def solution(mesh):
    return jax.shard_map(
        body,
        mesh=split_mesh(mesh),
        in_specs=(
            P(DP, SPACE, None),
            P(DP, None, SPACE),
            P(DP, SPACE),
            P(),
            P(),
            P(),
            P(),
            P(),
            P(DP, SPACE, None),
        ),
        out_specs=(P(DP, SPACE, None), P(DP, SPACE, None), P()),
        check_vma=False,
    )
```

```python
import functools
import math

import jax
import jax.numpy as jnp
from jax import lax
from jax.experimental import pallas as pl
from jax.experimental.pallas import tpu as pltpu
from jax.sharding import Mesh
from jax.sharding import PartitionSpec as P


DP = "y"
SPACE = ("z", "x", "core")
PLANE = ("y", "x", "core")
GROUP = 3
VMEM_BYTES = 32 << 20
PAR_ROWS = 64
COST_BYTES = 1 << 20


def split_mesh(mesh):
    dp, space = mesh.devices.shape
    return Mesh(mesh.devices.reshape(dp, space // 8, 4, 2), (DP,) + SPACE)


def shifted(array, by):
    length = lax.axis_size(SPACE)
    return lax.ppermute(array, SPACE, [(i, (i + by) % length) for i in range(length)])


def from_partner(array):
    length = lax.axis_size(SPACE)
    return lax.ppermute(array, SPACE, [(i, i ^ 1) for i in range(length)])


def settled(running, gain):
    inverse = lax.rsqrt(jnp.mean(running * running, axis=-1, keepdims=True) + 1e-05)
    scaled = running * inverse * gain
    return scaled / (1.0 + jnp.exp(-scaled))


def local_table(taps_ref):
    taps, _, rows = taps_ref.shape
    lowest = (lax.axis_index(SPACE) - 1) * rows
    ids = taps_ref[...].reshape(taps, rows)
    local = jnp.where(ids < 0, -4 * rows, ids - lowest)
    return jnp.concatenate([local, jnp.full((-taps % 8, rows), -1, jnp.int32)], axis=0).T


def pick(local, taps, blocks, select_ref, put, wait=None):
    rows = local.shape[0]
    places = lax.broadcasted_iota(jnp.int16, (rows, rows), 1)
    one, zero = jnp.ones((), jnp.bfloat16), jnp.zeros((), jnp.bfloat16)
    for tap in range(taps):
        column = jnp.broadcast_to(local[:, tap : tap + 1], (rows, 128))
        for b, (_, start) in enumerate(blocks):
            wanted = (column - start).astype(jnp.int16)
            wanted = jnp.concatenate([wanted] * (rows // 128), axis=1)
            select_ref[tap * rows : (tap + 1) * rows, b * rows : (b + 1) * rows] = jnp.where(
                wanted == places, one, zero
            )
    if wait is not None:
        wait()
    for first in range(0, taps, GROUP):
        part = select_ref[first * rows : (first + GROUP) * rows]
        picked = sum(
            jnp.dot(part[:, b * rows : (b + 1) * rows], block[...], preferred_element_type=jnp.float32)
            for b, (block, _) in enumerate(blocks)
        ).astype(jnp.bfloat16)
        for j in range(GROUP):
            put(first + j, picked[j * rows : (j + 1) * rows])


def pick_near(local, here, partner, select_ref, near_ref, wait=None):
    rows, chans = here.shape
    blocks = ((here, rows), (partner, 2 * rows * (1 - lax.axis_index("core"))))

    def put(tap, picked):
        near_ref[:, tap * chans : (tap + 1) * chans] = picked

    pick(local, near_ref.shape[1] // chans, blocks, select_ref, put, wait)


def convolved(local, before, after, near_ref, weight_ref, select_ref, picked_ref):
    rows, chans = before.shape
    across = jnp.where(lax.axis_index("core") == 1, after, before)
    taps = weight_ref.shape[0]

    def put(tap, picked):
        columns = slice(tap * chans, (tap + 1) * chans)
        picked_ref[:, columns] = near_ref[:, columns] + picked

    pick(local, taps, ((across, 2 * rows * lax.axis_index("core")),), select_ref, put)
    return jnp.dot(
        picked_ref[...],
        weight_ref[...].reshape(taps * chans, weight_ref.shape[2]),
        preferred_element_type=jnp.float32,
    )


def first_near_kernel(
    partner, taps_hbm, here_hbm, near_ref, local_ref, select_ref, taps_ref, here, taps_sem, here_sem
):
    taps_copy = pltpu.make_async_copy(taps_hbm, taps_ref, taps_sem)
    here_copy = pltpu.make_async_copy(here_hbm, here, here_sem)
    taps_copy.start()
    here_copy.start()
    taps_copy.wait()
    local = local_table(taps_ref)
    local_ref[...] = local
    pick_near(local, here, partner, select_ref, near_ref, here_copy.wait)


def first_far_kernel(
    local_ref, before, after, near_ref, weight_ref, gain_ref, parent_ref,
    middle_ref, select_ref, picked_ref,
):
    total = convolved(local_ref[...], before[...], after[...], near_ref, weight_ref, select_ref, picked_ref)
    rows = total.shape[0]
    middle_ref[:rows] = settled(total, gain_ref[...]).astype(middle_ref.dtype)
    ids = parent_ref[...] - lax.axis_index(SPACE) * PAR_ROWS
    ids = jnp.broadcast_to(ids.astype(jnp.float32), (middle_ref.shape[0] - rows, ids.shape[1]))
    middle_ref[rows:] = ids.astype(middle_ref.dtype)


def second_near_kernel(local_ref, here, partner, near_ref, select_ref):
    rows = local_ref.shape[0]
    pick_near(local_ref[...], here[:rows], partner[:rows], select_ref, near_ref)


def membership(ids, parents):
    return (lax.broadcasted_iota(jnp.int32, (parents, ids.shape[1]), 0) == ids).astype(jnp.float32)


def second_far_kernel(
    local_ref, before, after, near_ref, weight_ref, gain_ref, feature_ref, parent_ref,
    fine_ref, own_ref, sent_ref, share_ref, select_ref, picked_ref,
):
    rows, chans = feature_ref.shape
    total = convolved(local_ref[...], before[:rows], after[:rows], near_ref, weight_ref, select_ref, picked_ref)
    fine = feature_ref[...].astype(jnp.float32) + settled(total, gain_ref[...])
    fine = fine.astype(fine_ref.dtype)
    fine_ref[...] = fine
    half = own_ref.shape[0]
    member = membership(parent_ref[...] - lax.axis_index(SPACE) * half, 2 * half)
    sums = jnp.dot(member.astype(jnp.bfloat16), fine, preferred_element_type=jnp.float32)

    def tally(ids):
        return jnp.sum(membership(ids, 2 * half), axis=1, keepdims=True)

    tally_own = jnp.sum(member, axis=1, keepdims=True)
    tally_before = tally(before[rows:].astype(jnp.float32)[:1].astype(jnp.int32))[half:]
    tally_after = tally(after[rows:].astype(jnp.float32)[:1].astype(jnp.int32))[:half]
    count_own = jnp.maximum(tally_own[:half] + tally_before, 1.0)
    count_after = jnp.maximum(tally_own[half:] + tally_after, 1.0)
    own_ref[:, :chans] = sums[:half]
    own_ref[:, chans:] = jnp.broadcast_to(count_own, (half, own_ref.shape[1] - chans))
    sent_ref[...] = sums[half:]
    shares = sums / jnp.concatenate([count_own, count_after], axis=0)
    share_ref[...] = shares.astype(share_ref.dtype)


def gradient_kernel(share_ref, cotangent_ref, next_ref, grad_ref):
    grads_in = jnp.concatenate([cotangent_ref[...], next_ref[...]], axis=0)
    grad_ref[...] = lax.dot_general(
        share_ref[...], grads_in, (((0,), (0,)), ((), ())), preferred_element_type=jnp.float32
    ).astype(grad_ref.dtype)


def last_kernel(own_ref, moved_ref, down_ref, gathered_ref, coarse_ref, grad_ref):
    grad_ref[...] = gathered_ref[...].astype(grad_ref.dtype)
    chans = down_ref.shape[0]
    own = own_ref[...]
    pooled = ((own[:, :chans] + moved_ref[...]) / own[:, chans : chans + 1]).astype(jnp.bfloat16)
    coarse_ref[...] = jnp.dot(pooled, down_ref[...], preferred_element_type=jnp.float32).astype(coarse_ref.dtype)


def in_vmem(kernel, outs, inputs, name, scratch=(), flops=0, from_hbm=()):
    vmem = pl.BlockSpec(memory_space=pltpu.VMEM)
    return pl.pallas_call(
        kernel,
        out_shape=outs,
        in_specs=[vmem] * len(inputs) + [pl.BlockSpec(memory_space=pltpu.HBM)] * len(from_hbm),
        out_specs=jax.tree.map(lambda _: vmem, outs),
        scratch_shapes=scratch,
        compiler_params=pltpu.CompilerParams(vmem_limit_bytes=VMEM_BYTES),
        cost_estimate=pl.CostEstimate(flops=flops, bytes_accessed=COST_BYTES, transcendentals=0),
        name=name,
    )(*inputs, *[pltpu.with_memory_space_constraint(array, pltpu.HBM) for array in from_hbm])


def exchanged(pieces, axes):
    return lax.all_to_all(pieces, axes, 0, 0, tiled=True)


def plane_summed(local_grad):
    rows, cols = local_grad.shape
    plane = lax.axis_size(PLANE)
    return exchanged(local_grad.reshape(plane, rows // plane, cols), PLANE)


def space_summed(parts, scale):
    part = jnp.sum(parts.astype(jnp.float32), axis=0)
    copies = jnp.broadcast_to(part[None], (lax.axis_size("z"),) + part.shape)
    return jnp.sum(exchanged(copies, "z"), axis=0) * scale


def gathered(part):
    copies = jnp.broadcast_to(part.astype(jnp.bfloat16)[None], (lax.axis_size(PLANE),) + part.shape)
    return exchanged(copies, PLANE).reshape(-1, part.shape[1])


def body(
    features,
    neighbours,
    parents,
    conv_first,
    conv_second,
    gain_first,
    gain_second,
    down_weight,
    cotangent,
):
    field, grad_in = features[0], cotangent[0]
    _, taps, rows = neighbours.shape
    chans = field.shape[1]
    par_rows, out_chans = grad_in.shape
    bf16 = functools.partial(jax.ShapeDtypeStruct, dtype=jnp.bfloat16)
    f32 = functools.partial(jax.ShapeDtypeStruct, dtype=jnp.float32)
    product = 2 * taps * rows * chans * rows
    near_shape = bf16((rows, taps * chans))
    select = [pltpu.VMEM((taps * rows, 2 * rows), jnp.bfloat16)]
    select_and_picked = [
        pltpu.VMEM((taps * rows, rows), jnp.bfloat16),
        pltpu.VMEM((rows, taps * chans), jnp.bfloat16),
    ]
    after, before = shifted(field, -1), shifted(field, 1)
    near, local = in_vmem(
        first_near_kernel,
        (near_shape, jax.ShapeDtypeStruct((rows, taps + -taps % 8), jnp.int32)),
        (from_partner(field),),
        "first_near",
        select
        + [
            pltpu.VMEM((taps, 1, rows), jnp.int32),
            pltpu.VMEM((rows, chans), jnp.bfloat16),
            pltpu.SemaphoreType.DMA,
            pltpu.SemaphoreType.DMA,
        ],
        2 * product,
        (jnp.moveaxis(neighbours, 1, 0), field),
    )
    ready, near = lax.optimization_barrier((grad_in, near))
    next_grad = shifted(ready, -1)
    middle = in_vmem(
        first_far_kernel,
        bf16((rows + 16, chans)),
        (local, before, after, near, conv_first, gain_first[None], parents),
        "first_far", select_and_picked, 2 * product,
    )
    after, before = shifted(middle, -1), shifted(middle, 1)
    partner = from_partner(middle)
    near = in_vmem(
        second_near_kernel, near_shape, (local, middle, partner), "second_near", select, 2 * product
    )
    fine, own, sent, shares = in_vmem(
        second_far_kernel,
        (
            bf16((rows, chans)),
            f32((par_rows, chans + 128)),
            f32((par_rows, chans)),
            bf16((2 * par_rows, chans)),
        ),
        (
            local, before, after, near, conv_second, gain_second[None], field, parents,
        ),
        "second_far", select_and_picked, 2 * product,
    )
    local_grad = in_vmem(
        gradient_kernel, bf16((chans, out_chans)), (shares, grad_in, next_grad), "gradient"
    )
    worlds_all = lax.axis_size(DP)
    parents_all = par_rows * lax.axis_size(SPACE)
    part = space_summed(plane_summed(local_grad), 1.0 / math.sqrt(worlds_all * parents_all))
    sent, part = lax.optimization_barrier((sent, part))
    coarse, down_grad = in_vmem(
        last_kernel,
        (bf16((par_rows, out_chans)), f32((chans, out_chans))),
        (own, shifted(sent, 1), down_weight, gathered(part)),
        "coarse_and_grad",
    )
    return (fine[None], coarse[None], down_grad)


def solution(mesh):
    return jax.shard_map(
        body,
        mesh=split_mesh(mesh),
        in_specs=(
            P(DP, SPACE, None),
            P(DP, None, SPACE),
            P(DP, SPACE),
            P(),
            P(),
            P(),
            P(),
            P(),
            P(DP, SPACE, None),
        ),
        out_specs=(P(DP, SPACE, None), P(DP, SPACE, None), P()),
        check_vma=False,
    )
```

```python
import functools
import math

import jax
import jax.numpy as jnp
from jax import lax
from jax.experimental import pallas as pl
from jax.experimental.pallas import tpu as pltpu
from jax.sharding import Mesh
from jax.sharding import PartitionSpec as P


DP = "y"
SPACE = ("z", "x", "core")
PLANE = ("y", "x", "core")
GROUP = 9
VMEM_BYTES = 32 << 20
PAR_ROWS = 64
COST_BYTES = 1 << 20


def split_mesh(mesh):
    dp, space = mesh.devices.shape
    return Mesh(mesh.devices.reshape(dp, space // 8, 4, 2), (DP,) + SPACE)


def shifted(array, by):
    length = lax.axis_size(SPACE)
    return lax.ppermute(array, SPACE, [(i, (i + by) % length) for i in range(length)])


def from_partner(array):
    length = lax.axis_size(SPACE)
    return lax.ppermute(array, SPACE, [(i, i ^ 1) for i in range(length)])


def settled(running, gain):
    inverse = lax.rsqrt(jnp.mean(running * running, axis=-1, keepdims=True) + 1e-05)
    scaled = running * inverse * gain
    return scaled / (1.0 + jnp.exp(-scaled))


def local_table(taps_ref):
    taps, _, rows = taps_ref.shape
    lowest = (lax.axis_index(SPACE) - 1) * rows
    ids = taps_ref[...].reshape(taps, rows)
    local = jnp.where(ids < 0, -4 * rows, ids - lowest)
    return jnp.concatenate([local, jnp.full((-taps % 8, rows), -1, jnp.int32)], axis=0).T


def pick(local, taps, blocks, select_ref, put, wait=None):
    rows = local.shape[0]
    places = lax.broadcasted_iota(jnp.int16, (rows, rows), 1)
    one, zero = jnp.ones((), jnp.bfloat16), jnp.zeros((), jnp.bfloat16)
    for tap in range(taps):
        column = jnp.broadcast_to(local[:, tap : tap + 1], (rows, 128))
        for b, (_, start) in enumerate(blocks):
            wanted = (column - start).astype(jnp.int16)
            wanted = jnp.concatenate([wanted] * (rows // 128), axis=1)
            select_ref[tap * rows : (tap + 1) * rows, b * rows : (b + 1) * rows] = jnp.where(
                wanted == places, one, zero
            )
    if wait is not None:
        wait()
    for first in range(0, taps, GROUP):
        part = select_ref[first * rows : (first + GROUP) * rows]
        picked = sum(
            jnp.dot(part[:, b * rows : (b + 1) * rows], block[...], preferred_element_type=jnp.float32)
            for b, (block, _) in enumerate(blocks)
        ).astype(jnp.bfloat16)
        for j in range(GROUP):
            put(first + j, picked[j * rows : (j + 1) * rows])


def pick_near(local, here, partner, select_ref, near_ref, wait=None):
    rows, chans = here.shape
    blocks = ((here, rows), (partner, 2 * rows * (1 - lax.axis_index("core"))))

    def put(tap, picked):
        near_ref[:, tap * chans : (tap + 1) * chans] = picked

    pick(local, near_ref.shape[1] // chans, blocks, select_ref, put, wait)


def convolved(local, before, after, near_ref, weight_ref, select_ref, picked_ref):
    rows, chans = before.shape
    across = jnp.where(lax.axis_index("core") == 1, after, before)
    taps = weight_ref.shape[0]

    def put(tap, picked):
        columns = slice(tap * chans, (tap + 1) * chans)
        picked_ref[:, columns] = near_ref[:, columns] + picked

    pick(local, taps, ((across, 2 * rows * lax.axis_index("core")),), select_ref, put)
    return jnp.dot(
        picked_ref[...],
        weight_ref[...].reshape(taps * chans, weight_ref.shape[2]),
        preferred_element_type=jnp.float32,
    )


def first_near_kernel(
    partner, taps_hbm, here_hbm, near_ref, local_ref, select_ref, taps_ref, here, taps_sem, here_sem
):
    taps_copy = pltpu.make_async_copy(taps_hbm, taps_ref, taps_sem)
    here_copy = pltpu.make_async_copy(here_hbm, here, here_sem)
    taps_copy.start()
    here_copy.start()
    taps_copy.wait()
    local = local_table(taps_ref)
    local_ref[...] = local
    pick_near(local, here, partner, select_ref, near_ref, here_copy.wait)


def first_far_kernel(
    local_ref, before, after, near_ref, weight_ref, gain_ref, parent_ref,
    middle_ref, select_ref, picked_ref,
):
    total = convolved(local_ref[...], before[...], after[...], near_ref, weight_ref, select_ref, picked_ref)
    rows = total.shape[0]
    middle_ref[:rows] = settled(total, gain_ref[...]).astype(middle_ref.dtype)
    ids = parent_ref[...] - lax.axis_index(SPACE) * PAR_ROWS
    ids = jnp.broadcast_to(ids.astype(jnp.float32), (middle_ref.shape[0] - rows, ids.shape[1]))
    middle_ref[rows:] = ids.astype(middle_ref.dtype)


def second_near_kernel(local_ref, here, partner, near_ref, select_ref):
    rows = local_ref.shape[0]
    pick_near(local_ref[...], here[:rows], partner[:rows], select_ref, near_ref)


def membership(ids, parents):
    return (lax.broadcasted_iota(jnp.int32, (parents, ids.shape[1]), 0) == ids).astype(jnp.float32)


def second_far_kernel(
    local_ref, before, after, near_ref, weight_ref, gain_ref, feature_ref, parent_ref,
    fine_ref, own_ref, sent_ref, share_ref, select_ref, picked_ref,
):
    rows, chans = feature_ref.shape
    total = convolved(local_ref[...], before[:rows], after[:rows], near_ref, weight_ref, select_ref, picked_ref)
    fine = feature_ref[...].astype(jnp.float32) + settled(total, gain_ref[...])
    fine = fine.astype(fine_ref.dtype)
    fine_ref[...] = fine
    half = own_ref.shape[0]
    member = membership(parent_ref[...] - lax.axis_index(SPACE) * half, 2 * half)
    sums = jnp.dot(member.astype(jnp.bfloat16), fine, preferred_element_type=jnp.float32)

    def tally(ids):
        return jnp.sum(membership(ids, 2 * half), axis=1, keepdims=True)

    tally_own = jnp.sum(member, axis=1, keepdims=True)
    tally_before = tally(before[rows:].astype(jnp.float32)[:1].astype(jnp.int32))[half:]
    tally_after = tally(after[rows:].astype(jnp.float32)[:1].astype(jnp.int32))[:half]
    count_own = jnp.maximum(tally_own[:half] + tally_before, 1.0)
    count_after = jnp.maximum(tally_own[half:] + tally_after, 1.0)
    own_ref[:, :chans] = sums[:half]
    own_ref[:, chans:] = jnp.broadcast_to(count_own, (half, own_ref.shape[1] - chans))
    sent_ref[...] = sums[half:]
    shares = sums / jnp.concatenate([count_own, count_after], axis=0)
    share_ref[...] = shares.astype(share_ref.dtype)


def gradient_kernel(share_ref, cotangent_ref, next_ref, grad_ref):
    grads_in = jnp.concatenate([cotangent_ref[...], next_ref[...]], axis=0)
    grad_ref[...] = lax.dot_general(
        share_ref[...], grads_in, (((0,), (0,)), ((), ())), preferred_element_type=jnp.float32
    ).astype(grad_ref.dtype)


def last_kernel(own_ref, moved_ref, down_ref, gathered_ref, coarse_ref, grad_ref):
    grad_ref[...] = gathered_ref[...].astype(grad_ref.dtype)
    chans = down_ref.shape[0]
    own = own_ref[...]
    pooled = ((own[:, :chans] + moved_ref[...]) / own[:, chans : chans + 1]).astype(jnp.bfloat16)
    coarse_ref[...] = jnp.dot(pooled, down_ref[...], preferred_element_type=jnp.float32).astype(coarse_ref.dtype)


def in_vmem(kernel, outs, inputs, name, scratch=(), flops=0, from_hbm=()):
    vmem = pl.BlockSpec(memory_space=pltpu.VMEM)
    return pl.pallas_call(
        kernel,
        out_shape=outs,
        in_specs=[vmem] * len(inputs) + [pl.BlockSpec(memory_space=pltpu.HBM)] * len(from_hbm),
        out_specs=jax.tree.map(lambda _: vmem, outs),
        scratch_shapes=scratch,
        compiler_params=pltpu.CompilerParams(vmem_limit_bytes=VMEM_BYTES),
        cost_estimate=pl.CostEstimate(flops=flops, bytes_accessed=COST_BYTES, transcendentals=0),
        name=name,
    )(*inputs, *[pltpu.with_memory_space_constraint(array, pltpu.HBM) for array in from_hbm])


def exchanged(pieces, axes):
    return lax.all_to_all(pieces, axes, 0, 0, tiled=True)


def plane_summed(local_grad):
    rows, cols = local_grad.shape
    plane = lax.axis_size(PLANE)
    return exchanged(local_grad.reshape(plane, rows // plane, cols), PLANE)


def space_summed(parts, scale):
    part = jnp.sum(parts.astype(jnp.float32), axis=0)
    copies = jnp.broadcast_to(part[None], (lax.axis_size("z"),) + part.shape)
    return jnp.sum(exchanged(copies, "z"), axis=0) * scale


def gathered(part):
    copies = jnp.broadcast_to(part.astype(jnp.bfloat16)[None], (lax.axis_size(PLANE),) + part.shape)
    return exchanged(copies, PLANE).reshape(-1, part.shape[1])


def body(
    features,
    neighbours,
    parents,
    conv_first,
    conv_second,
    gain_first,
    gain_second,
    down_weight,
    cotangent,
):
    field, grad_in = features[0], cotangent[0]
    _, taps, rows = neighbours.shape
    chans = field.shape[1]
    par_rows, out_chans = grad_in.shape
    bf16 = functools.partial(jax.ShapeDtypeStruct, dtype=jnp.bfloat16)
    f32 = functools.partial(jax.ShapeDtypeStruct, dtype=jnp.float32)
    product = 2 * taps * rows * chans * rows
    near_shape = bf16((rows, taps * chans))
    select = [pltpu.VMEM((taps * rows, 2 * rows), jnp.bfloat16)]
    select_and_picked = [
        pltpu.VMEM((taps * rows, rows), jnp.bfloat16),
        pltpu.VMEM((rows, taps * chans), jnp.bfloat16),
    ]
    after, before = shifted(field, -1), shifted(field, 1)
    near, local = in_vmem(
        first_near_kernel,
        (near_shape, jax.ShapeDtypeStruct((rows, taps + -taps % 8), jnp.int32)),
        (from_partner(field),),
        "first_near",
        select
        + [
            pltpu.VMEM((taps, 1, rows), jnp.int32),
            pltpu.VMEM((rows, chans), jnp.bfloat16),
            pltpu.SemaphoreType.DMA,
            pltpu.SemaphoreType.DMA,
        ],
        2 * product,
        (jnp.moveaxis(neighbours, 1, 0), field),
    )
    ready, near = lax.optimization_barrier((grad_in, near))
    next_grad = shifted(ready, -1)
    middle = in_vmem(
        first_far_kernel,
        bf16((rows + 16, chans)),
        (local, before, after, near, conv_first, gain_first[None], parents),
        "first_far", select_and_picked, 2 * product,
    )
    after, before = shifted(middle, -1), shifted(middle, 1)
    partner = from_partner(middle)
    near = in_vmem(
        second_near_kernel, near_shape, (local, middle, partner), "second_near", select, 2 * product
    )
    fine, own, sent, shares = in_vmem(
        second_far_kernel,
        (
            bf16((rows, chans)),
            f32((par_rows, chans + 128)),
            f32((par_rows, chans)),
            bf16((2 * par_rows, chans)),
        ),
        (
            local, before, after, near, conv_second, gain_second[None], field, parents,
        ),
        "second_far", select_and_picked, 2 * product,
    )
    local_grad = in_vmem(
        gradient_kernel, bf16((chans, out_chans)), (shares, grad_in, next_grad), "gradient"
    )
    worlds_all = lax.axis_size(DP)
    parents_all = par_rows * lax.axis_size(SPACE)
    part = space_summed(plane_summed(local_grad), 1.0 / math.sqrt(worlds_all * parents_all))
    sent, part = lax.optimization_barrier((sent, part))
    coarse, down_grad = in_vmem(
        last_kernel,
        (bf16((par_rows, out_chans)), f32((chans, out_chans))),
        (own, shifted(sent, 1), down_weight, gathered(part)),
        "coarse_and_grad",
    )
    return (fine[None], coarse[None], down_grad)


def solution(mesh):
    return jax.shard_map(
        body,
        mesh=split_mesh(mesh),
        in_specs=(
            P(DP, SPACE, None),
            P(DP, None, SPACE),
            P(DP, SPACE),
            P(),
            P(),
            P(),
            P(),
            P(),
            P(DP, SPACE, None),
        ),
        out_specs=(P(DP, SPACE, None), P(DP, SPACE, None), P()),
        check_vma=False,
    )
```

```python
import functools
import math

import jax
import jax.numpy as jnp
from jax import lax
from jax.experimental import pallas as pl
from jax.experimental.pallas import tpu as pltpu
from jax.sharding import Mesh
from jax.sharding import PartitionSpec as P


DP = "y"
SPACE = ("z", "x", "core")
PLANE = ("y", "x", "core")
GROUP = 9
VMEM_BYTES = 32 << 20
PAR_ROWS = 64
COST_BYTES = 1 << 20


def split_mesh(mesh):
    dp, space = mesh.devices.shape
    return Mesh(mesh.devices.reshape(dp, space // 8, 4, 2), (DP,) + SPACE)


def shifted(array, by):
    length = lax.axis_size(SPACE)
    return lax.ppermute(array, SPACE, [(i, (i + by) % length) for i in range(length)])


def from_partner(array):
    length = lax.axis_size(SPACE)
    return lax.ppermute(array, SPACE, [(i, i ^ 1) for i in range(length)])


def settled(running, gain):
    inverse = lax.rsqrt(jnp.mean(running * running, axis=-1, keepdims=True) + 1e-05)
    scaled = running * inverse * gain
    return scaled / (1.0 + jnp.exp(-scaled))


def local_table(taps_ref):
    taps, _, rows = taps_ref.shape
    lowest = (lax.axis_index(SPACE) - 1) * rows
    ids = taps_ref[...].reshape(taps, rows)
    local = jnp.where(ids < 0, -4 * rows, ids - lowest)
    return jnp.concatenate([local, jnp.full((-taps % 8, rows), -1, jnp.int32)], axis=0).T


def pick(local, taps, blocks, select_ref, put, wait=None):
    rows = local.shape[0]
    places = lax.broadcasted_iota(jnp.int16, (rows, rows), 1)
    one, zero = jnp.ones((), jnp.bfloat16), jnp.zeros((), jnp.bfloat16)
    for tap in range(taps):
        column = jnp.broadcast_to(local[:, tap : tap + 1], (rows, 128))
        for b, (_, start) in enumerate(blocks):
            wanted = (column - start).astype(jnp.int16)
            wanted = jnp.concatenate([wanted] * (rows // 128), axis=1)
            select_ref[tap * rows : (tap + 1) * rows, b * rows : (b + 1) * rows] = jnp.where(
                wanted == places, one, zero
            )
    if wait is not None:
        wait()
    for first in range(0, taps, GROUP):
        part = select_ref[first * rows : (first + GROUP) * rows]
        picked = sum(
            jnp.dot(part[:, b * rows : (b + 1) * rows], block[...], preferred_element_type=jnp.float32)
            for b, (block, _) in enumerate(blocks)
        ).astype(jnp.bfloat16)
        for j in range(GROUP):
            put(first + j, picked[j * rows : (j + 1) * rows])


def pick_near(local, here, partner, select_ref, near_ref, wait=None):
    rows, chans = here.shape
    blocks = ((here, rows), (partner, 2 * rows * (1 - lax.axis_index("core"))))

    def put(tap, picked):
        near_ref[:, tap * chans : (tap + 1) * chans] = picked

    pick(local, near_ref.shape[1] // chans, blocks, select_ref, put, wait)


def convolved(local, before, after, near_ref, weight_ref, select_ref, picked_ref):
    rows, chans = before.shape
    across = jnp.where(lax.axis_index("core") == 1, after, before)
    taps = weight_ref.shape[0]

    def put(tap, picked):
        columns = slice(tap * chans, (tap + 1) * chans)
        picked_ref[:, columns] = near_ref[:, columns] + picked

    pick(local, taps, ((across, 2 * rows * lax.axis_index("core")),), select_ref, put)
    return jnp.dot(
        picked_ref[...],
        weight_ref[...].reshape(taps * chans, weight_ref.shape[2]),
        preferred_element_type=jnp.float32,
    )


def first_near_kernel(
    partner, taps_hbm, here_hbm, near_ref, local_ref, select_ref, taps_ref, here, taps_sem, here_sem
):
    taps_copy = pltpu.make_async_copy(taps_hbm, taps_ref, taps_sem)
    here_copy = pltpu.make_async_copy(here_hbm, here, here_sem)
    taps_copy.start()
    here_copy.start()
    taps_copy.wait()
    local = local_table(taps_ref)
    local_ref[...] = local
    pick_near(local, here, partner, select_ref, near_ref, here_copy.wait)


def first_far_kernel(
    local_ref, before, after, near_ref, weight_ref, gain_ref, parent_ref,
    middle_ref, select_ref, picked_ref,
):
    total = convolved(local_ref[...], before[...], after[...], near_ref, weight_ref, select_ref, picked_ref)
    rows = total.shape[0]
    middle_ref[:rows] = settled(total, gain_ref[...]).astype(middle_ref.dtype)
    ids = parent_ref[...] - lax.axis_index(SPACE) * PAR_ROWS
    ids = jnp.broadcast_to(ids.astype(jnp.float32), (middle_ref.shape[0] - rows, ids.shape[1]))
    middle_ref[rows:] = ids.astype(middle_ref.dtype)


def second_near_kernel(local_ref, here, partner, near_ref, select_ref):
    rows = local_ref.shape[0]
    pick_near(local_ref[...], here[:rows], partner[:rows], select_ref, near_ref)


def membership(ids, parents):
    return (lax.broadcasted_iota(jnp.int32, (parents, ids.shape[1]), 0) == ids).astype(jnp.float32)


def second_far_kernel(
    local_ref, before, after, near_ref, weight_ref, gain_ref, feature_ref, parent_ref,
    fine_hbm, own_ref, sent_ref, share_ref, select_ref, picked_ref, fine_ref, fine_sem,
):
    rows, chans = feature_ref.shape
    total = convolved(local_ref[...], before[:rows], after[:rows], near_ref, weight_ref, select_ref, picked_ref)
    fine = feature_ref[...].astype(jnp.float32) + settled(total, gain_ref[...])
    fine = fine.astype(fine_ref.dtype)
    fine_ref[...] = fine
    copy = pltpu.make_async_copy(fine_ref, fine_hbm, fine_sem)
    copy.start()
    half = own_ref.shape[0]
    member = membership(parent_ref[...] - lax.axis_index(SPACE) * half, 2 * half)
    sums = jnp.dot(member.astype(jnp.bfloat16), fine, preferred_element_type=jnp.float32)

    def tally(ids):
        return jnp.sum(membership(ids, 2 * half), axis=1, keepdims=True)

    tally_own = jnp.sum(member, axis=1, keepdims=True)
    tally_before = tally(before[rows:].astype(jnp.float32)[:1].astype(jnp.int32))[half:]
    tally_after = tally(after[rows:].astype(jnp.float32)[:1].astype(jnp.int32))[:half]
    count_own = jnp.maximum(tally_own[:half] + tally_before, 1.0)
    count_after = jnp.maximum(tally_own[half:] + tally_after, 1.0)
    own_ref[:, :chans] = sums[:half]
    own_ref[:, chans:] = jnp.broadcast_to(count_own, (half, own_ref.shape[1] - chans))
    sent_ref[...] = sums[half:]
    shares = sums / jnp.concatenate([count_own, count_after], axis=0)
    share_ref[...] = shares.astype(share_ref.dtype)
    copy.wait()


def gradient_kernel(share_ref, cotangent_ref, next_ref, grad_ref):
    grads_in = jnp.concatenate([cotangent_ref[...], next_ref[...]], axis=0)
    grad_ref[...] = lax.dot_general(
        share_ref[...], grads_in, (((0,), (0,)), ((), ())), preferred_element_type=jnp.float32
    ).astype(grad_ref.dtype)


def last_kernel(own_ref, moved_ref, down_ref, gathered_ref, coarse_ref, grad_ref):
    grad_ref[...] = gathered_ref[...].astype(grad_ref.dtype)
    chans = down_ref.shape[0]
    own = own_ref[...]
    pooled = ((own[:, :chans] + moved_ref[...]) / own[:, chans : chans + 1]).astype(jnp.bfloat16)
    coarse_ref[...] = jnp.dot(pooled, down_ref[...], preferred_element_type=jnp.float32).astype(coarse_ref.dtype)


def in_vmem(kernel, outs, inputs, name, scratch=(), flops=0, from_hbm=(), to_hbm=0):
    vmem = pl.BlockSpec(memory_space=pltpu.VMEM)
    return pl.pallas_call(
        kernel,
        out_shape=outs,
        in_specs=[vmem] * len(inputs) + [pl.BlockSpec(memory_space=pltpu.HBM)] * len(from_hbm),
        out_specs=([pl.BlockSpec(memory_space=pl.ANY)] * to_hbm + [vmem] * (len(outs) - to_hbm))
        if isinstance(outs, tuple)
        else vmem,
        scratch_shapes=scratch,
        compiler_params=pltpu.CompilerParams(vmem_limit_bytes=VMEM_BYTES),
        cost_estimate=pl.CostEstimate(flops=flops, bytes_accessed=COST_BYTES, transcendentals=0),
        name=name,
    )(*inputs, *[pltpu.with_memory_space_constraint(array, pltpu.HBM) for array in from_hbm])


def exchanged(pieces, axes):
    return lax.all_to_all(pieces, axes, 0, 0, tiled=True)


def plane_summed(local_grad):
    rows, cols = local_grad.shape
    plane = lax.axis_size(PLANE)
    return exchanged(local_grad.reshape(plane, rows // plane, cols), PLANE)


def space_summed(parts, scale):
    part = jnp.sum(parts.astype(jnp.float32), axis=0)
    copies = jnp.broadcast_to(part[None], (lax.axis_size("z"),) + part.shape)
    return jnp.sum(exchanged(copies, "z"), axis=0) * scale


def gathered(part):
    copies = jnp.broadcast_to(part.astype(jnp.bfloat16)[None], (lax.axis_size(PLANE),) + part.shape)
    return exchanged(copies, PLANE).reshape(-1, part.shape[1])


def body(
    features,
    neighbours,
    parents,
    conv_first,
    conv_second,
    gain_first,
    gain_second,
    down_weight,
    cotangent,
):
    field, grad_in = features[0], cotangent[0]
    _, taps, rows = neighbours.shape
    chans = field.shape[1]
    par_rows, out_chans = grad_in.shape
    bf16 = functools.partial(jax.ShapeDtypeStruct, dtype=jnp.bfloat16)
    f32 = functools.partial(jax.ShapeDtypeStruct, dtype=jnp.float32)
    product = 2 * taps * rows * chans * rows
    near_shape = bf16((rows, taps * chans))
    select = [pltpu.VMEM((taps * rows, 2 * rows), jnp.bfloat16)]
    select_and_picked = [
        pltpu.VMEM((taps * rows, rows), jnp.bfloat16),
        pltpu.VMEM((rows, taps * chans), jnp.bfloat16),
    ]
    after, before = shifted(field, -1), shifted(field, 1)
    near, local = in_vmem(
        first_near_kernel,
        (near_shape, jax.ShapeDtypeStruct((rows, taps + -taps % 8), jnp.int32)),
        (from_partner(field),),
        "first_near",
        select
        + [
            pltpu.VMEM((taps, 1, rows), jnp.int32),
            pltpu.VMEM((rows, chans), jnp.bfloat16),
            pltpu.SemaphoreType.DMA,
            pltpu.SemaphoreType.DMA,
        ],
        2 * product,
        (jnp.moveaxis(neighbours, 1, 0), field),
    )
    ready, near = lax.optimization_barrier((grad_in, near))
    next_grad = shifted(ready, -1)
    middle = in_vmem(
        first_far_kernel,
        bf16((rows + 16, chans)),
        (local, before, after, near, conv_first, gain_first[None], parents),
        "first_far", select_and_picked, 2 * product,
    )
    after, before = shifted(middle, -1), shifted(middle, 1)
    partner = from_partner(middle)
    near = in_vmem(
        second_near_kernel, near_shape, (local, middle, partner), "second_near", select, 2 * product
    )
    fine, own, sent, shares = in_vmem(
        second_far_kernel,
        (
            bf16((rows, chans)),
            f32((par_rows, chans + 128)),
            f32((par_rows, chans)),
            bf16((2 * par_rows, chans)),
        ),
        (
            local, before, after, near, conv_second, gain_second[None], field, parents,
        ),
        "second_far",
        select_and_picked + [pltpu.VMEM((rows, chans), jnp.bfloat16), pltpu.SemaphoreType.DMA],
        2 * product,
        to_hbm=1,
    )
    local_grad = in_vmem(
        gradient_kernel, bf16((chans, out_chans)), (shares, grad_in, next_grad), "gradient"
    )
    worlds_all = lax.axis_size(DP)
    parents_all = par_rows * lax.axis_size(SPACE)
    part = space_summed(plane_summed(local_grad), 1.0 / math.sqrt(worlds_all * parents_all))
    sent, part = lax.optimization_barrier((sent, part))
    coarse, down_grad = in_vmem(
        last_kernel,
        (bf16((par_rows, out_chans)), f32((chans, out_chans))),
        (own, shifted(sent, 1), down_weight, gathered(part)),
        "coarse_and_grad",
    )
    return (fine[None], coarse[None], down_grad)


def solution(mesh):
    return jax.shard_map(
        body,
        mesh=split_mesh(mesh),
        in_specs=(
            P(DP, SPACE, None),
            P(DP, None, SPACE),
            P(DP, SPACE),
            P(),
            P(),
            P(),
            P(),
            P(),
            P(DP, SPACE, None),
        ),
        out_specs=(P(DP, SPACE, None), P(DP, SPACE, None), P()),
        check_vma=False,
    )
```

```python
import functools
import math

import jax
import jax.numpy as jnp
from jax import lax
from jax.experimental import pallas as pl
from jax.experimental.pallas import tpu as pltpu
from jax.sharding import Mesh
from jax.sharding import PartitionSpec as P


DP = "y"
SPACE = ("z", "x", "core")
PLANE = ("y", "x", "core")
GROUP = 9
VMEM_BYTES = 32 << 20
PAR_ROWS = 64
COST_BYTES = 1 << 20


def split_mesh(mesh):
    dp, space = mesh.devices.shape
    return Mesh(mesh.devices.reshape(dp, space // 8, 4, 2), (DP,) + SPACE)


def shifted(array, by):
    length = lax.axis_size(SPACE)
    return lax.ppermute(array, SPACE, [(i, (i + by) % length) for i in range(length)])


def from_partner(array):
    length = lax.axis_size(SPACE)
    return lax.ppermute(array, SPACE, [(i, i ^ 1) for i in range(length)])


def settled(running, gain):
    inverse = lax.rsqrt(jnp.mean(running * running, axis=-1, keepdims=True) + 1e-05)
    scaled = running * inverse * gain
    return scaled / (1.0 + jnp.exp(-scaled))


def local_table(taps_ref):
    taps, _, rows = taps_ref.shape
    lowest = (lax.axis_index(SPACE) - 1) * rows
    ids = taps_ref[...].reshape(taps, rows)
    local = jnp.where(ids < 0, -4 * rows, ids - lowest)
    return jnp.concatenate([local, jnp.full((-taps % 8, rows), -1, jnp.int32)], axis=0).T


def pick(local, taps, blocks, select_ref, put, wait=None):
    rows = local.shape[0]
    places = lax.broadcasted_iota(jnp.int16, (rows, rows), 1)
    one, zero = jnp.ones((), jnp.bfloat16), jnp.zeros((), jnp.bfloat16)
    for tap in range(taps):
        column = jnp.broadcast_to(local[:, tap : tap + 1], (rows, 128))
        for b, (_, start) in enumerate(blocks):
            wanted = (column - start).astype(jnp.int16)
            wanted = jnp.concatenate([wanted] * (rows // 128), axis=1)
            select_ref[tap * rows : (tap + 1) * rows, b * rows : (b + 1) * rows] = jnp.where(
                wanted == places, one, zero
            )
    if wait is not None:
        wait()
    for first in range(0, taps, GROUP):
        part = select_ref[first * rows : (first + GROUP) * rows]
        picked = sum(
            jnp.dot(part[:, b * rows : (b + 1) * rows], block[...], preferred_element_type=jnp.float32)
            for b, (block, _) in enumerate(blocks)
        ).astype(jnp.bfloat16)
        for j in range(GROUP):
            put(first + j, picked[j * rows : (j + 1) * rows])


def pick_near(local, here, partner, select_ref, near_ref, wait=None):
    rows, chans = here.shape
    blocks = ((here, rows), (partner, 2 * rows * (1 - lax.axis_index("core"))))

    def put(tap, picked):
        near_ref[:, tap * chans : (tap + 1) * chans] = picked

    pick(local, near_ref.shape[1] // chans, blocks, select_ref, put, wait)


def convolved(local, before, after, near_ref, weight_ref, select_ref, picked_ref):
    rows, chans = before.shape
    across = jnp.where(lax.axis_index("core") == 1, after, before)
    taps = weight_ref.shape[0]

    def put(tap, picked):
        columns = slice(tap * chans, (tap + 1) * chans)
        picked_ref[:, columns] = near_ref[:, columns] + picked

    pick(local, taps, ((across, 2 * rows * lax.axis_index("core")),), select_ref, put)
    return jnp.dot(
        picked_ref[...],
        weight_ref[...].reshape(taps * chans, weight_ref.shape[2]),
        preferred_element_type=jnp.float32,
    )


def first_near_kernel(
    partner, taps_hbm, here_hbm, near_ref, local_ref, select_ref, taps_ref, here, taps_sem, here_sem
):
    taps_copy = pltpu.make_async_copy(taps_hbm, taps_ref, taps_sem)
    here_copy = pltpu.make_async_copy(here_hbm, here, here_sem)
    taps_copy.start()
    here_copy.start()
    taps_copy.wait()
    local = local_table(taps_ref)
    local_ref[...] = local
    pick_near(local, here, partner, select_ref, near_ref, here_copy.wait)


def first_far_kernel(
    local_ref, before, after, near_ref, weight_ref, gain_ref, parent_ref,
    middle_ref, select_ref, picked_ref,
):
    total = convolved(local_ref[...], before[...], after[...], near_ref, weight_ref, select_ref, picked_ref)
    rows = total.shape[0]
    middle_ref[:rows] = settled(total, gain_ref[...]).astype(middle_ref.dtype)
    ids = parent_ref[...] - lax.axis_index(SPACE) * PAR_ROWS
    ids = jnp.broadcast_to(ids.astype(jnp.float32), (middle_ref.shape[0] - rows, ids.shape[1]))
    middle_ref[rows:] = ids.astype(middle_ref.dtype)


def second_near_kernel(local_ref, here, partner, near_ref, select_ref):
    rows = local_ref.shape[0]
    pick_near(local_ref[...], here[:rows], partner[:rows], select_ref, near_ref)


def membership(ids, parents):
    return (lax.broadcasted_iota(jnp.int32, (parents, ids.shape[1]), 0) == ids).astype(jnp.float32)


def second_far_kernel(
    local_ref, before, after, near_ref, weight_ref, gain_ref, feature_ref, parent_ref,
    fine_ref, own_ref, sent_ref, share_ref, select_ref, picked_ref,
):
    rows, chans = feature_ref.shape
    total = convolved(local_ref[...], before[:rows], after[:rows], near_ref, weight_ref, select_ref, picked_ref)
    fine = feature_ref[...].astype(jnp.float32) + settled(total, gain_ref[...])
    fine = fine.astype(fine_ref.dtype)
    fine_ref[...] = fine
    half = own_ref.shape[0]
    member = membership(parent_ref[...] - lax.axis_index(SPACE) * half, 2 * half)
    sums = jnp.dot(member.astype(jnp.bfloat16), fine, preferred_element_type=jnp.float32)

    def tally(ids):
        return jnp.sum(membership(ids, 2 * half), axis=1, keepdims=True)

    tally_own = jnp.sum(member, axis=1, keepdims=True)
    tally_before = tally(before[rows:].astype(jnp.float32)[:1].astype(jnp.int32))[half:]
    tally_after = tally(after[rows:].astype(jnp.float32)[:1].astype(jnp.int32))[:half]
    count_own = jnp.maximum(tally_own[:half] + tally_before, 1.0)
    count_after = jnp.maximum(tally_own[half:] + tally_after, 1.0)
    own_ref[:, :chans] = sums[:half]
    own_ref[:, chans:] = jnp.broadcast_to(count_own, (half, own_ref.shape[1] - chans))
    sent_ref[...] = sums[half:].astype(sent_ref.dtype)
    shares = sums / jnp.concatenate([count_own, count_after], axis=0)
    share_ref[...] = shares.astype(share_ref.dtype)


def gradient_kernel(share_ref, cotangent_ref, next_ref, grad_ref):
    grads_in = jnp.concatenate([cotangent_ref[...], next_ref[...]], axis=0)
    grad_ref[...] = lax.dot_general(
        share_ref[...], grads_in, (((0,), (0,)), ((), ())), preferred_element_type=jnp.float32
    ).astype(grad_ref.dtype)


def last_kernel(own_ref, moved_ref, down_ref, gathered_ref, coarse_ref, grad_ref):
    grad_ref[...] = gathered_ref[...].astype(grad_ref.dtype)
    chans = down_ref.shape[0]
    own = own_ref[...]
    pooled = ((own[:, :chans] + moved_ref[...].astype(jnp.float32)) / own[:, chans : chans + 1]).astype(jnp.bfloat16)
    coarse_ref[...] = jnp.dot(pooled, down_ref[...], preferred_element_type=jnp.float32).astype(coarse_ref.dtype)


def in_vmem(kernel, outs, inputs, name, scratch=(), flops=0, from_hbm=()):
    vmem = pl.BlockSpec(memory_space=pltpu.VMEM)
    return pl.pallas_call(
        kernel,
        out_shape=outs,
        in_specs=[vmem] * len(inputs) + [pl.BlockSpec(memory_space=pltpu.HBM)] * len(from_hbm),
        out_specs=jax.tree.map(lambda _: vmem, outs),
        scratch_shapes=scratch,
        compiler_params=pltpu.CompilerParams(vmem_limit_bytes=VMEM_BYTES),
        cost_estimate=pl.CostEstimate(flops=flops, bytes_accessed=COST_BYTES, transcendentals=0),
        name=name,
    )(*inputs, *[pltpu.with_memory_space_constraint(array, pltpu.HBM) for array in from_hbm])


def exchanged(pieces, axes):
    return lax.all_to_all(pieces, axes, 0, 0, tiled=True)


def plane_summed(local_grad):
    rows, cols = local_grad.shape
    plane = lax.axis_size(PLANE)
    return exchanged(local_grad.reshape(plane, rows // plane, cols), PLANE)


def space_summed(parts, scale):
    part = jnp.sum(parts.astype(jnp.float32), axis=0)
    copies = jnp.broadcast_to(part[None], (lax.axis_size("z"),) + part.shape)
    return jnp.sum(exchanged(copies, "z"), axis=0) * scale


def gathered(part):
    copies = jnp.broadcast_to(part.astype(jnp.bfloat16)[None], (lax.axis_size(PLANE),) + part.shape)
    return exchanged(copies, PLANE).reshape(-1, part.shape[1])


def body(
    features,
    neighbours,
    parents,
    conv_first,
    conv_second,
    gain_first,
    gain_second,
    down_weight,
    cotangent,
):
    field, grad_in = features[0], cotangent[0]
    _, taps, rows = neighbours.shape
    chans = field.shape[1]
    par_rows, out_chans = grad_in.shape
    bf16 = functools.partial(jax.ShapeDtypeStruct, dtype=jnp.bfloat16)
    f32 = functools.partial(jax.ShapeDtypeStruct, dtype=jnp.float32)
    product = 2 * taps * rows * chans * rows
    near_shape = bf16((rows, taps * chans))
    select = [pltpu.VMEM((taps * rows, 2 * rows), jnp.bfloat16)]
    select_and_picked = [
        pltpu.VMEM((taps * rows, rows), jnp.bfloat16),
        pltpu.VMEM((rows, taps * chans), jnp.bfloat16),
    ]
    after, before = shifted(field, -1), shifted(field, 1)
    near, local = in_vmem(
        first_near_kernel,
        (near_shape, jax.ShapeDtypeStruct((rows, taps + -taps % 8), jnp.int32)),
        (from_partner(field),),
        "first_near",
        select
        + [
            pltpu.VMEM((taps, 1, rows), jnp.int32),
            pltpu.VMEM((rows, chans), jnp.bfloat16),
            pltpu.SemaphoreType.DMA,
            pltpu.SemaphoreType.DMA,
        ],
        2 * product,
        (jnp.moveaxis(neighbours, 1, 0), field),
    )
    ready, near = lax.optimization_barrier((grad_in, near))
    next_grad = shifted(ready, -1)
    middle = in_vmem(
        first_far_kernel,
        bf16((rows + 16, chans)),
        (local, before, after, near, conv_first, gain_first[None], parents),
        "first_far", select_and_picked, 2 * product,
    )
    after, before = shifted(middle, -1), shifted(middle, 1)
    partner = from_partner(middle)
    near = in_vmem(
        second_near_kernel, near_shape, (local, middle, partner), "second_near", select, 2 * product
    )
    fine, own, sent, shares = in_vmem(
        second_far_kernel,
        (
            bf16((rows, chans)),
            f32((par_rows, chans + 128)),
            bf16((par_rows, chans)),
            bf16((2 * par_rows, chans)),
        ),
        (
            local, before, after, near, conv_second, gain_second[None], field, parents,
        ),
        "second_far", select_and_picked, 2 * product,
    )
    local_grad = in_vmem(
        gradient_kernel, bf16((chans, out_chans)), (shares, grad_in, next_grad), "gradient"
    )
    worlds_all = lax.axis_size(DP)
    parents_all = par_rows * lax.axis_size(SPACE)
    part = space_summed(plane_summed(local_grad), 1.0 / math.sqrt(worlds_all * parents_all))
    sent, part = lax.optimization_barrier((sent, part))
    coarse, down_grad = in_vmem(
        last_kernel,
        (bf16((par_rows, out_chans)), f32((chans, out_chans))),
        (own, shifted(sent, 1), down_weight, gathered(part)),
        "coarse_and_grad",
    )
    return (fine[None], coarse[None], down_grad)


def solution(mesh):
    return jax.shard_map(
        body,
        mesh=split_mesh(mesh),
        in_specs=(
            P(DP, SPACE, None),
            P(DP, None, SPACE),
            P(DP, SPACE),
            P(),
            P(),
            P(),
            P(),
            P(),
            P(DP, SPACE, None),
        ),
        out_specs=(P(DP, SPACE, None), P(DP, SPACE, None), P()),
        check_vma=False,
    )
```
